32 devices in a mesh: groups: 2 (over x), row: 16 (over z, y, core).
Axes of the slice: x: 2, y: 2, z: 4, core: 2. Of those that a mesh axis runs over, the one named last changes fastest.
Arguments:
- basis: float32 [32768, 512], P(('groups', 'row')), parts along dimension 0, may hold values from -0.0625 to 0.0625
- weights: bfloat16 [32, 2048, 4096], P(('groups', 'row')), parts along dimension 0, may hold values from -6 to 6
Outputs:
- rotated: bfloat16 [1024, 8192], P(('groups', 'row')), parts along dimension 0
The draws below stay inside these ranges and needn't reach their ends.
There are 2 independent parts, one for each index of `groups`. The reference program is written for one: setup_inputs(seed, part) draws one part's arguments, and reference() takes and returns one part's arrays. A program takes and returns all parts, laid end to end along the dimension named above; each array names one. Nothing has to cross between parts.
All inputs are finite; a program needn't handle non-finite values.
Results may differ from the reference program's by a relative error of at most 0.001.
Values may be sent and summed in bfloat16 or wider, within the bound.
No kernel may reach another device: no remote copies, remote signals or barrier semaphores. Data moves between devices by JAX's collectives and lax.ppermute only.
A program may use at most 128 MiB of HBM per device.

```python
import jax
import jax.numpy as jnp
from jax import lax

D = 16384
C = 8192
R = 512
MB = 8
QB = 2
DB = 2048
CQ = 4096
N_ROW = 16


def with_spikes(values, stream_key, source, target, parts, factor):
    def block_of(axis_at):
        return (jnp.arange(values.shape[axis_at]) // (values.shape[axis_at] // parts)).reshape((-1,) + (1,) * (values.ndim - 1 - axis_at))

    near = jax.random.permutation(stream_key, parts)[block_of(target)]
    other_side = (block_of(target) + parts // 2) % parts
    return jnp.where((block_of(source) == near) | (block_of(source) == other_side), factor * values, values)


def block_levels(own_key, dims, shards, smallest, top_value):
    def one(dim, parts):
        steps = jax.random.uniform(jax.random.fold_in(jax.random.fold_in(own_key, 6), dim), (parts,), jnp.float32, smallest / len(shards), top_value / len(shards))
        return jnp.repeat(jnp.exp(steps), dims[dim] // parts).reshape((-1,) + (1,) * (len(dims) - dim - 1))

    loudness = one(*shards[0])
    for cut in shards[1:]:
        loudness = loudness * one(*cut)
    return loudness


def scatter_about(rng, dims, deviation, bound, split=(), dtype=jnp.bfloat16):
    values = deviation * jax.random.normal(rng, dims, jnp.float32)
    if split:
        values = values * block_levels(rng, dims, split, -0.22, 0.18)
    return jnp.clip(values, -bound, bound).astype(dtype)


def heavy_noise(stream_key, shape, scale, bound, pieces, heavy, held_as=jnp.bfloat16):
    entries = scale * jax.random.normal(stream_key, shape, jnp.float32)
    if pieces:
        entries = entries * block_levels(stream_key, shape, pieces, -0.22, 0.18)
    return jnp.clip(with_spikes(entries, jax.random.fold_in(stream_key, 3), *heavy), -bound, bound).astype(held_as)


def setup_inputs(seed: int = 0, part: int = 0) -> dict:
    key_list = jax.random.split(jax.random.key(seed), 3)
    part_splits = jax.random.split(jax.random.fold_in(key_list[2], part), 3)
    basis = heavy_noise(part_splits[0], (D, R), D ** -0.5, 0.0625, ((0, 16),), (0, 1, 16, 2.0), jnp.float32)
    weights = scatter_about(part_splits[1], (N_ROW, DB, CQ), 1.0, 6.0, ((0, 16),))
    return {"basis": basis, "weights": weights}


def reference(basis, weights):
    grid = weights.reshape(MB, QB, DB, CQ)
    slab = jnp.transpose(grid, (0, 2, 1, 3)).reshape(D, C)
    product = jnp.dot(basis.T, slab.astype(jnp.float32), precision=lax.Precision.HIGHEST, preferred_element_type=jnp.float32)
    return product.astype(jnp.bfloat16)
```

```python
import functools

import jax
import jax.numpy as jnp
from jax import lax
from jax.experimental import pallas as pl
from jax.experimental.pallas import tpu as pltpu
from jax.sharding import PartitionSpec as P

LANES = 128
SCALE_ROWS = 16
HALF_SPAN = 125.0
SPAN = 250.0
TINY = 2.0**-110
MIB = 1 << 20


def column_bound(values):
    top = jnp.maximum(jnp.max(jnp.abs(values), axis=0, keepdims=True), TINY)
    return (top * 1.008).astype(jnp.bfloat16).astype(jnp.float32)


def encode(values, bound):
    level = jnp.exp2(jnp.abs(values) * (SPAN / bound) - HALF_SPAN)
    return jnp.where(values < 0, -level, level).astype(jnp.bfloat16)


def decode(coded, bound):
    coded = coded.astype(jnp.float32)
    size = (jnp.log2(jnp.abs(coded)) + HALF_SPAN) * (bound * (1.0 / SPAN))
    return jnp.where(coded < 0, -size, size)


def reversed_bits(value, bits):
    out = 0
    for bit in range(bits):
        out |= (value >> bit & 1) << (bits - 1 - bit)
    return out


def split_places(order, bits):
    stay = list(range(1 << bits))
    stages = []
    for bit in order:
        leave = [p for p in stay if reversed_bits(p, bits) >> bit & 1]
        stay = [p for p in stay if not reversed_bits(p, bits) >> bit & 1]
        stages.append((leave, stay))
    return stages


def put_message(message_ref, values, tiles, count):
    bounds = []
    for tile in range(tiles):
        sent = values[tile]
        bound = column_bound(sent)
        message_ref[tile * count : (tile + 1) * count, :] = encode(sent, bound)
        bounds.append(bound)
    bounds.append(jnp.zeros((SCALE_ROWS - tiles, LANES), jnp.float32))
    message_ref[tiles * count :, :] = jnp.concatenate(bounds, axis=0).astype(jnp.bfloat16)


def prepare_kernel(blocks, bits, place_ref, basis_ref, out_ref, turned):
    turned[...] = basis_ref[...].T
    rows = turned.shape[0]
    step = rows // blocks
    for place in range(blocks):
        source = jnp.bitwise_xor(place_ref[0], reversed_bits(place, bits))
        part = turned[pl.ds(pl.multiple_of(source * step, step), step), :]
        high = part.astype(jnp.bfloat16)
        low = (part - high.astype(jnp.float32)).astype(jnp.bfloat16)
        out_ref[place * step : (place + 1) * step, :] = high
        out_ref[rows + place * step : rows + (place + 1) * step, :] = low


def prepare(basis, place, blocks, bits):
    depth, rows = basis.shape
    wide = min(depth, 256)
    return pl.pallas_call(
        functools.partial(prepare_kernel, blocks, bits),
        grid_spec=pltpu.PrefetchScalarGridSpec(
            num_scalar_prefetch=1,
            grid=(depth // wide,),
            in_specs=[pl.BlockSpec((wide, rows), lambda i, s: (i, 0))],
            out_specs=pl.BlockSpec((2 * rows, wide), lambda i, s: (0, i)),
            scratch_shapes=[pltpu.VMEM((rows, wide), jnp.float32)],
        ),
        out_shape=jax.ShapeDtypeStruct((2 * rows, depth), jnp.bfloat16),
        cost_estimate=pl.CostEstimate(
            flops=2 * depth * rows, bytes_accessed=8 * depth * rows, transcendentals=0
        ),
        name="split_basis",
    )(place, basis)


def product_kernel(pieces, step, leave, stay, place_ref, *refs):
    left = refs[:pieces]
    right = refs[pieces : 2 * pieces]
    message_ref, kept_ref = refs[2 * pieces :]
    total = None
    for a_ref, w_ref in zip(left, right):
        part = jnp.dot(a_ref[...], w_ref[0], preferred_element_type=jnp.float32)
        total = part if total is None else total + part
    rows = total.shape[0] // 2
    total = total[:rows] + total[rows:]
    tiles = total.shape[1] // LANES
    sent = []
    count = len(stay) * step
    for tile in range(tiles):
        column = total[:, tile * LANES : (tile + 1) * LANES]
        sent.append(jnp.concatenate([column[p * step : (p + 1) * step] for p in leave], axis=0))
        for slot, p in enumerate(stay):
            at = tile * count + slot * step
            kept_ref[at : at + step, :] = column[p * step : (p + 1) * step]
    put_message(message_ref, sent, tiles, len(leave) * step)


def product(left, weights, column, start, width, wide, step, leave, stay):
    pieces = len(left)
    rows2, depth = left[0].shape
    steps = width // wide
    tiles = wide // LANES
    sent_rows = tiles * len(leave) * step + SCALE_ROWS
    kept_rows = tiles * len(stay) * step
    first = start // wide

    def weight_spec(distance):
        return pl.BlockSpec(
            (1, depth, wide), lambda j, s: (0, jnp.bitwise_xor(s[0], distance), first + j)
        )

    return pl.pallas_call(
        functools.partial(product_kernel, pieces, step, leave, stay),
        grid_spec=pltpu.PrefetchScalarGridSpec(
            num_scalar_prefetch=1,
            grid=(steps,),
            in_specs=[
                pl.BlockSpec((rows2, depth), lambda j, s: (0, 0), pipeline_mode=pl.Buffered(1))
                for _ in left
            ]
            + [weight_spec(distance) for distance in range(pieces)],
            out_specs=[
                pl.BlockSpec((sent_rows, LANES), lambda j, s: (j, 0)),
                pl.BlockSpec((kept_rows, LANES), lambda j, s: (j, 0)),
            ],
        ),
        out_shape=[
            jax.ShapeDtypeStruct((steps * sent_rows, LANES), jnp.bfloat16),
            jax.ShapeDtypeStruct((steps * kept_rows, LANES), jnp.float32),
        ],
        compiler_params=pltpu.CompilerParams(vmem_limit_bytes=40 * MIB),
        cost_estimate=pl.CostEstimate(
            flops=2 * rows2 * depth * pieces * width,
            bytes_accessed=2 * depth * pieces * width + 4 * rows2 * width,
            transcendentals=rows2 * width // 4,
        ),
        name="product",
    )(column, *left, *([weights] * pieces))


def received(message_ref, kept_ref, tile, tiles, count):
    bounds = message_ref[tiles * count :, :].astype(jnp.float32)
    coded = message_ref[tile * count : (tile + 1) * count, :]
    return kept_ref[tile * count : (tile + 1) * count, :] + decode(coded, bounds[tile : tile + 1])


def middle_kernel(tiles, step, old, leave, stay, message_ref, kept_ref, out_ref, next_ref):
    sent = []
    count = len(stay) * step
    for tile in range(tiles):
        column = received(message_ref, kept_ref, tile, tiles, len(old) * step)
        blocks = {p: column[i * step : (i + 1) * step] for i, p in enumerate(old)}
        sent.append(jnp.concatenate([blocks[p] for p in leave], axis=0))
        for slot, p in enumerate(stay):
            at = tile * count + slot * step
            next_ref[at : at + step, :] = blocks[p]
    put_message(out_ref, sent, tiles, len(leave) * step)


def middle(message, kept, width, wide, step, old, leave, stay):
    steps = width // wide
    tiles = wide // LANES
    in_rows = tiles * len(old) * step
    sent_rows = tiles * len(leave) * step + SCALE_ROWS
    kept_rows = tiles * len(stay) * step
    return pl.pallas_call(
        functools.partial(middle_kernel, tiles, step, old, leave, stay),
        grid=(steps,),
        in_specs=[
            pl.BlockSpec((in_rows + SCALE_ROWS, LANES), lambda j: (j, 0)),
            pl.BlockSpec((in_rows, LANES), lambda j: (j, 0)),
        ],
        out_specs=[
            pl.BlockSpec((sent_rows, LANES), lambda j: (j, 0)),
            pl.BlockSpec((kept_rows, LANES), lambda j: (j, 0)),
        ],
        out_shape=[
            jax.ShapeDtypeStruct((steps * sent_rows, LANES), jnp.bfloat16),
            jax.ShapeDtypeStruct((steps * kept_rows, LANES), jnp.float32),
        ],
        cost_estimate=pl.CostEstimate(
            flops=20 * steps * in_rows * LANES,
            bytes_accessed=9 * steps * in_rows * LANES,
            transcendentals=2 * steps * in_rows * LANES,
        ),
        name="add_and_split",
    )(message, kept)


def last_kernel(tiles, pieces, place_ref, message_ref, kept_ref, *refs):
    outs = refs[:pieces]
    whole = refs[pieces]
    count = whole.shape[0]
    share = count // pieces
    for tile in range(tiles):
        whole[:, tile * LANES : (tile + 1) * LANES] = received(
            message_ref, kept_ref, tile, tiles, count
        )
    for distance in range(pieces):
        owner = jnp.bitwise_xor(place_ref[0], distance)
        rows = whole[pl.ds(pl.multiple_of(owner * share, share), share), :]
        outs[distance][...] = rows.astype(jnp.bfloat16)


def last(message, kept, column, width, wide, step, pieces):
    steps = width // wide
    tiles = wide // LANES
    in_rows = tiles * step
    share = step // pieces
    return pl.pallas_call(
        functools.partial(last_kernel, tiles, pieces),
        grid_spec=pltpu.PrefetchScalarGridSpec(
            num_scalar_prefetch=1,
            grid=(steps,),
            in_specs=[
                pl.BlockSpec((in_rows + SCALE_ROWS, LANES), lambda j, s: (j, 0)),
                pl.BlockSpec((in_rows, LANES), lambda j, s: (j, 0)),
            ],
            out_specs=[pl.BlockSpec((share, wide), lambda j, s: (0, j))] * pieces,
            scratch_shapes=[pltpu.VMEM((step, wide), jnp.float32)],
        ),
        out_shape=[jax.ShapeDtypeStruct((share, width), jnp.bfloat16)] * pieces,
        cost_estimate=pl.CostEstimate(
            flops=10 * steps * in_rows * LANES,
            bytes_accessed=8 * steps * in_rows * LANES,
            transcendentals=steps * in_rows * LANES,
        ),
        name="add_last",
    )(column, message, kept)


def swapped(block, apart):
    count = lax.axis_size("row")
    return lax.ppermute(block, "row", [(i, i ^ apart) for i in range(count)])


def on_device(basis, weights):
    axis_len = lax.axis_size("row")
    depth, rows = basis.shape
    pieces = weights.shape[1] // depth
    blocks = axis_len // pieces
    bits = blocks.bit_length() - 1
    piece_bits = pieces.bit_length() - 1
    step = rows // blocks
    width = weights.shape[2]
    me = lax.axis_index("row").astype(jnp.int32)
    column = jnp.bitwise_and(me, pieces - 1)
    place = jnp.right_shift(me, piece_bits)[None]
    column_at = column[None]

    own = prepare(basis, place, blocks, bits)
    left = [own] + [swapped(own, distance) for distance in range(1, pieces)]

    chunk = width // 4
    wide = min(chunk, 512)
    plain = list(range(bits))
    orders = [plain] * 4
    if bits > 1:
        orders[1] = [1, 0] + plain[2:]

    finished = []
    for index, order in enumerate(orders):
        stages = split_places(order, bits)
        message, kept = product(
            left, weights, column_at, index * chunk, chunk, wide, step, *stages[0]
        )
        for number, bit in enumerate(order):
            message = swapped(message, pieces << bit)
            if number + 1 < bits:
                message, kept = middle(
                    message, kept, chunk, wide, step, stages[number][1], *stages[number + 1]
                )
        parts = last(message, kept, column_at, chunk, wide, step, pieces)
        finished.append(
            [parts[0]] + [swapped(parts[distance], distance) for distance in range(1, pieces)]
        )
    out = [jnp.concatenate(parts, axis=1) for parts in zip(*finished)]
    for bit in range(piece_bits):
        odd = jnp.right_shift(column, bit) & 1 == 1
        out = [jnp.where(odd, out[q ^ 1 << bit], out[q]) for q in range(pieces)]
    return jnp.concatenate(out, axis=1)


def solution(mesh):
    in_specs = (P(("groups", "row"), None), P(("groups", "row"), None, None))
    out_specs = P(("groups", "row"), None)
    return jax.shard_map(
        on_device, mesh=mesh, in_specs=in_specs, out_specs=out_specs, check_vma=False
    )
```

```python
import functools

import jax
import jax.numpy as jnp
from jax import lax
from jax.experimental import pallas as pl
from jax.experimental.pallas import tpu as pltpu
from jax.sharding import PartitionSpec as P

LANES = 128
SCALE_ROWS = 16
COLUMNS = 256
HALF_SPAN = 125.0
SPAN = 250.0
TINY = 2.0**-110
MIB = 1 << 20

ORDER = [
    (0, 0), (1, 0), (2, 0), (0, 1), (3, 0), (1, 1), (0, 2), (2, 1),
    (0, 3), (2, 2), (3, 1), (1, 2), (2, 3), (3, 2), (1, 3), (3, 3),
]


def column_bound(values):
    top = jnp.maximum(jnp.max(jnp.abs(values), axis=0, keepdims=True), TINY)
    return (top * 1.008).astype(jnp.bfloat16).astype(jnp.float32)


def encode(values, bound):
    level = jnp.exp2(jnp.abs(values) * (SPAN / bound) - HALF_SPAN)
    return jnp.where(values < 0, -level, level).astype(jnp.bfloat16)


def decode(coded, bound):
    coded = coded.astype(jnp.float32)
    size = (jnp.log2(jnp.abs(coded)) + HALF_SPAN) * (bound * (1.0 / SPAN))
    return jnp.where(coded < 0, -size, size)


def reversed_bits(value, bits):
    out = 0
    for bit in range(bits):
        out |= (value >> bit & 1) << (bits - 1 - bit)
    return out


def split_places(order, bits):
    stay = list(range(1 << bits))
    stages = []
    for bit in order:
        leave = [p for p in stay if reversed_bits(p, bits) >> bit & 1]
        stay = [p for p in stay if not reversed_bits(p, bits) >> bit & 1]
        stages.append((leave, stay))
    return stages


def scale_rows(tiles):
    return -(-tiles // SCALE_ROWS) * SCALE_ROWS


def put_bounds(message_ref, bounds, count):
    tiles = len(bounds)
    spare = scale_rows(tiles) - tiles
    if spare:
        bounds = bounds + [jnp.zeros((spare, LANES), jnp.float32)]
    message_ref[tiles * count :, :] = jnp.concatenate(bounds, axis=0).astype(jnp.bfloat16)


def put_tile(message_ref, kept_ref, tile, blocks, step, leave, stay):
    sent = jnp.concatenate([blocks[p] for p in leave], axis=0)
    bound = column_bound(sent)
    count = len(leave) * step
    message_ref[tile * count : (tile + 1) * count, :] = encode(sent, bound)
    for slot, p in enumerate(stay):
        at = (tile * len(stay) + slot) * step
        kept_ref[at : at + step, :] = blocks[p]
    return bound


def call(kernel, name, ins, outs, after, scratch=(), limit=4, cost=(0, 0, 0)):
    count = len(ins)

    def run(*refs):
        kernel(*refs[:count], *refs[count + len(after) :])

    vmem = pl.BlockSpec(memory_space=pltpu.VMEM)
    return pl.pallas_call(
        run,
        in_specs=[pl.BlockSpec(memory_space=pltpu.SMEM)]
        + [vmem] * (count - 1)
        + [pl.BlockSpec(memory_space=pl.ANY)] * len(after),
        out_specs=[vmem] * len(outs),
        out_shape=outs,
        scratch_shapes=scratch,
        compiler_params=pltpu.CompilerParams(vmem_limit_bytes=limit * MIB),
        cost_estimate=pl.CostEstimate(
            flops=cost[0], bytes_accessed=cost[1], transcendentals=cost[2]
        ),
        name=name,
    )(*ins, *after)


def prepare_kernel(blocks, bits, place_ref, basis_ref, out_ref, turned):
    depth, rows = basis_ref.shape
    step = rows // blocks
    wide = min(depth, 256)
    for at in range(0, depth, wide):
        turned[:, at : at + wide] = basis_ref[at : at + wide, :].T
    for place in range(blocks):
        source = jnp.bitwise_xor(place_ref[1], reversed_bits(place, bits))
        part = turned[pl.ds(pl.multiple_of(source * step, step), step), :]
        high = part.astype(jnp.bfloat16)
        low = (part - high.astype(jnp.float32)).astype(jnp.bfloat16)
        out_ref[place * step : (place + 1) * step, :] = high
        out_ref[rows + place * step : rows + (place + 1) * step, :] = low


def prepare(basis, places, blocks, bits):
    depth, rows = basis.shape
    return call(
        functools.partial(prepare_kernel, blocks, bits),
        "split_basis",
        [places, basis],
        [jax.ShapeDtypeStruct((2 * rows, depth), jnp.bfloat16)],
        [],
        [pltpu.VMEM((rows, depth), jnp.float32)],
        limit=6,
        cost=(2 * depth * rows, 8 * depth * rows, 0),
    )[0]


def product_kernel(pieces, start, width, step, leave, stay, place_ref, w_ref, *refs):
    left = refs[:pieces]
    message_ref, kept_ref = refs[pieces:]
    depth = left[0].shape[1]
    wide = min(width, COLUMNS)
    bounds = []
    for at in range(0, width, wide):
        total = None
        for distance, a_ref in enumerate(left):
            owner = jnp.bitwise_xor(place_ref[0], distance)
            rows = pl.ds(pl.multiple_of(owner * depth, depth), depth)
            part = jnp.dot(
                a_ref[...],
                w_ref[0, rows, start + at : start + at + wide],
                preferred_element_type=jnp.float32,
            )
            total = part if total is None else total + part
        half = total.shape[0] // 2
        total = total[:half] + total[half:]
        for lane in range(0, wide, LANES):
            column = total[:, lane : lane + LANES]
            blocks = {p: column[p * step : (p + 1) * step] for p in leave + stay}
            tile = (at + lane) // LANES
            bounds.append(put_tile(message_ref, kept_ref, tile, blocks, step, leave, stay))
    put_bounds(message_ref, bounds, len(leave) * step)


def outputs(width, step, leave, stay):
    tiles = width // LANES
    sent = tiles * len(leave) * step + scale_rows(tiles)
    return [
        jax.ShapeDtypeStruct((sent, LANES), jnp.bfloat16),
        jax.ShapeDtypeStruct((tiles * len(stay) * step, LANES), jnp.float32),
    ]


def product(left, weights, places, start, width, step, leave, stay, after):
    rows2, depth = left[0].shape
    return call(
        functools.partial(product_kernel, len(left), start, width, step, leave, stay),
        "product",
        [places, weights, *left],
        outputs(width, step, leave, stay),
        after,
        limit=8,
        cost=(
            2 * rows2 * depth * len(left) * width,
            2 * depth * len(left) * width + 4 * rows2 * width,
            rows2 * width // 4,
        ),
    )


def received(message_ref, kept_ref, tile, tiles, count):
    coded = message_ref[tile * count : (tile + 1) * count, :]
    group = tile // SCALE_ROWS * SCALE_ROWS
    at = tiles * count + group
    bounds = message_ref[at : at + SCALE_ROWS, :].astype(jnp.float32)
    bound = bounds[tile - group : tile - group + 1]
    return kept_ref[tile * count : (tile + 1) * count, :] + decode(coded, bound)


def middle_kernel(tiles, step, old, leave, stay, place_ref, message_ref, kept_ref, out_ref, next_ref):
    bounds = []
    for tile in range(tiles):
        column = received(message_ref, kept_ref, tile, tiles, len(old) * step)
        blocks = {p: column[i * step : (i + 1) * step] for i, p in enumerate(old)}
        bounds.append(put_tile(out_ref, next_ref, tile, blocks, step, leave, stay))
    put_bounds(out_ref, bounds, len(leave) * step)


def middle(message, kept, places, width, step, old, leave, stay, after):
    size = width * len(old) * step
    return call(
        functools.partial(middle_kernel, width // LANES, step, old, leave, stay),
        "add_and_split",
        [places, message, kept],
        outputs(width, step, leave, stay),
        after,
        cost=(20 * size, 9 * size, 2 * size),
    )


def last_kernel(tiles, pieces, place_ref, message_ref, kept_ref, *refs):
    outs = refs[:pieces]
    whole = refs[pieces]
    count = whole.shape[0]
    share = count // pieces
    for tile in range(tiles):
        whole[:, tile * LANES : (tile + 1) * LANES] = received(
            message_ref, kept_ref, tile, tiles, count
        )
    for distance in range(pieces):
        owner = jnp.bitwise_xor(place_ref[0], distance)
        rows = whole[pl.ds(pl.multiple_of(owner * share, share), share), :]
        outs[distance][...] = rows.astype(jnp.bfloat16)


def last(message, kept, places, width, step, pieces, after):
    size = width * step
    share = jax.ShapeDtypeStruct((step // pieces, width), jnp.bfloat16)
    return call(
        functools.partial(last_kernel, width // LANES, pieces),
        "add_last",
        [places, message, kept],
        [share] * pieces,
        after,
        [pltpu.VMEM((step, width), jnp.float32)],
        cost=(10 * size, 8 * size, size),
    )


def lay_kernel(pieces, width, place_ref, *refs):
    out_ref = refs[-1]
    at = 0
    for first in range(0, len(refs) - 1, pieces):
        for distance in range(pieces):
            part = refs[first + distance]
            owner = jnp.bitwise_xor(place_ref[0], distance)
            columns = pl.ds(pl.multiple_of(owner * width + at, LANES), part.shape[1])
            out_ref[:, columns] = part[...]
        at += part.shape[1]


def lay(parts, places, pieces, width):
    flat = [part for chunk in parts for part in chunk]
    rows = flat[0].shape[0]
    return call(
        functools.partial(lay_kernel, pieces, width),
        "lay_out",
        [places, *flat],
        [jax.ShapeDtypeStruct((rows, pieces * width), jnp.bfloat16)],
        [],
        cost=(0, 4 * rows * pieces * width, 0),
    )[0]


def swapped(block, apart):
    count = lax.axis_size("row")
    return lax.ppermute(block, "row", [(i, i ^ apart) for i in range(count)])


def on_device(basis, weights):
    axis_len = lax.axis_size("row")
    depth, rows = basis.shape
    pieces = weights.shape[1] // depth
    blocks = axis_len // pieces
    bits = blocks.bit_length() - 1
    piece_bits = pieces.bit_length() - 1
    step = rows // blocks
    width = weights.shape[2]
    me = lax.axis_index("row").astype(jnp.int32)
    column = jnp.bitwise_and(me, pieces - 1)
    places = jnp.stack([column, jnp.right_shift(me, piece_bits)])

    own = prepare(basis, places, blocks, bits)
    left = [own] + [swapped(own, distance) for distance in range(1, pieces)]

    chunk = width // 4
    plain = list(range(bits))
    orders = [plain] * 4
    if bits > 1:
        orders[1] = [1, 0] + plain[2:]
    stages = [split_places(order, bits) for order in orders]

    state = {}
    after = []
    finished = {}
    for index, number in ORDER:
        order = orders[index]
        if number == 0:
            out = product(
                left, weights, places, index * chunk, chunk, step, *stages[index][0], after
            )
        elif number < bits:
            message, kept = state[index]
            old = stages[index][number - 1][1]
            out = middle(message, kept, places, chunk, step, old, *stages[index][number], after)
        else:
            message, kept = state[index]
            out = last(message, kept, places, chunk, step, pieces, after)
            finished[index] = [out[0]] + [swapped(out[d], d) for d in range(1, pieces)]
            after = [out[0]]
            continue
        state[index] = swapped(out[0], pieces << order[number]), out[1]
        after = [out[1]]
    return lay([finished[index] for index in range(4)], places, pieces, width)


def solution(mesh):
    in_specs = (P(("groups", "row"), None), P(("groups", "row"), None, None))
    out_specs = P(("groups", "row"), None)
    return jax.shard_map(
        on_device, mesh=mesh, in_specs=in_specs, out_specs=out_specs, check_vma=False
    )
```

```python
import functools

import jax
import jax.numpy as jnp
from jax import lax
from jax.experimental import pallas as pl
from jax.experimental.pallas import tpu as pltpu
from jax.sharding import PartitionSpec as P

LANES = 128
SCALE_ROWS = 16
COLUMNS = 256
HALF_SPAN = 125.0
SPAN = 250.0
TINY = 2.0**-110
MIB = 1 << 20

CHUNKS = [(4, (0, 1, 2)), (4, (1, 0, 2)), (4, (0, 1, 2)), (4, (0, 1, 2))]
PARTS = 16
EARLY = 2
ORDER = [
    (0, 0), (1, 0), (2, 0), (0, 1), (3, 0), (1, 1), (0, 2), (2, 1),
    (0, 3), (2, 2), (3, 1), (1, 2), (2, 3), (3, 2), (1, 3), (3, 3),
]


def column_bound(values):
    top = jnp.maximum(jnp.max(jnp.abs(values), axis=0, keepdims=True), TINY)
    return (top * 1.008).astype(jnp.bfloat16).astype(jnp.float32)


def encode(values, bound):
    level = jnp.exp2(jnp.abs(values) * (SPAN / bound) - HALF_SPAN)
    return jnp.where(values < 0, -level, level).astype(jnp.bfloat16)


def decode(coded, bound):
    coded = coded.astype(jnp.float32)
    size = (jnp.log2(jnp.abs(coded)) + HALF_SPAN) * (bound * (1.0 / SPAN))
    return jnp.where(coded < 0, -size, size)


def reversed_bits(value, bits):
    out = 0
    for bit in range(bits):
        out |= (value >> bit & 1) << (bits - 1 - bit)
    return out


def split_places(order, bits):
    stay = list(range(1 << bits))
    stages = []
    for bit in order:
        leave = [p for p in stay if reversed_bits(p, bits) >> bit & 1]
        stay = [p for p in stay if not reversed_bits(p, bits) >> bit & 1]
        stages.append((leave, stay))
    return stages


def scale_rows(tiles):
    return -(-tiles // SCALE_ROWS) * SCALE_ROWS


def put_bounds(message_ref, bounds, count):
    tiles = len(bounds)
    spare = scale_rows(tiles) - tiles
    if spare:
        bounds = bounds + [jnp.zeros((spare, LANES), jnp.float32)]
    message_ref[tiles * count :, :] = jnp.concatenate(bounds, axis=0).astype(jnp.bfloat16)


def put_tile(message_ref, kept_ref, tile, blocks, step, leave, stay):
    sent = jnp.concatenate([blocks[p] for p in leave], axis=0)
    bound = column_bound(sent)
    count = len(leave) * step
    message_ref[tile * count : (tile + 1) * count, :] = encode(sent, bound)
    for slot, p in enumerate(stay):
        at = (tile * len(stay) + slot) * step
        kept_ref[at : at + step, :] = blocks[p]
    return bound


def call(kernel, name, ins, outs, after, scratch=(), limit=4, cost=(0, 0, 0), far=0):
    count = len(ins)

    def run(*refs):
        kernel(*refs[:count], *refs[count + len(after) :])

    vmem = pl.BlockSpec(memory_space=pltpu.VMEM)
    near = count - far
    ins = ins[:near] + [pltpu.with_memory_space_constraint(x, pltpu.HBM) for x in ins[near:]]
    return pl.pallas_call(
        run,
        in_specs=[pl.BlockSpec(memory_space=pltpu.SMEM)]
        + [vmem] * (count - 1 - far)
        + [pl.BlockSpec(memory_space=pltpu.HBM)] * far
        + [pl.BlockSpec(memory_space=pl.ANY)] * len(after),
        out_specs=[vmem] * len(outs),
        out_shape=outs,
        scratch_shapes=scratch,
        compiler_params=pltpu.CompilerParams(vmem_limit_bytes=limit * MIB),
        cost_estimate=pl.CostEstimate(
            flops=cost[0], bytes_accessed=cost[1], transcendentals=cost[2]
        ),
        name=name,
    )(*ins, *after)


def prepare_kernel(blocks, bits, wide, place_ref, basis_ref, out_ref, held, turned, sems):
    depth, rows = basis_ref.shape
    step = rows // blocks
    copies = []
    for index, at in enumerate(range(0, depth, wide)):
        part = pl.ds(at, wide)
        copies.append(
            pltpu.make_async_copy(basis_ref.at[part, :], held.at[part, :], sems.at[index])
        )
        copies[-1].start()
    for index, at in enumerate(range(0, depth, wide)):
        copies[index].wait()
        turned[:, at : at + wide] = held[at : at + wide, :].T
        for place in range(blocks):
            source = jnp.bitwise_xor(place_ref[1], reversed_bits(place, bits))
            part = turned[pl.ds(pl.multiple_of(source * step, step), step), at : at + wide]
            high = part.astype(jnp.bfloat16)
            low = (part - high.astype(jnp.float32)).astype(jnp.bfloat16)
            out_ref[place * step : (place + 1) * step, at : at + wide] = high
            out_ref[rows + place * step : rows + (place + 1) * step, at : at + wide] = low


def prepare(basis, places, blocks, bits):
    depth, rows = basis.shape
    wide = min(depth, COLUMNS)
    return call(
        functools.partial(prepare_kernel, blocks, bits, wide),
        "split_basis",
        [places, basis],
        [jax.ShapeDtypeStruct((2 * rows, depth), jnp.bfloat16)],
        [],
        [
            pltpu.VMEM((depth, rows), jnp.float32),
            pltpu.VMEM((rows, depth), jnp.float32),
            pltpu.SemaphoreType.DMA((depth // wide,)),
        ],
        limit=10,
        cost=(2 * depth * rows, 8 * depth * rows, 0),
        far=1,
    )[0]


def spans(width, wide):
    return [(at, min(wide, width - at)) for at in range(0, width, wide)]


def halves_added(product):
    half = product.shape[0] // 2
    return product[:half] + product[half:]


def early_kernel(pieces, width, place_ref, own_ref, w_ref, near_ref, partial_ref, sems):
    depth = own_ref.shape[1]
    full = w_ref.shape[2]
    copies = []

    def bring(distance, at, wide):
        owner = jnp.bitwise_xor(place_ref[0], distance)
        rows = pl.ds(pl.multiple_of(owner * depth, depth), depth)
        copy = pltpu.make_async_copy(
            w_ref.at[0, rows, pl.ds(at, wide)],
            near_ref.at[pl.ds(distance * depth, depth), pl.ds(at, wide)],
            sems.at[len(copies)],
        )
        copy.start()
        copies.append(copy)

    first = spans(width, COLUMNS)
    for at, wide in first:
        bring(0, at, wide)
    for index, (at, wide) in enumerate(first):
        copies[index].wait()
        if index == 0:
            if full > width:
                bring(0, width, full - width)
            for distance in range(1, pieces):
                bring(distance, 0, full)
        part = jnp.dot(
            own_ref[...],
            near_ref[0:depth, at : at + wide],
            preferred_element_type=jnp.float32,
        )
        partial_ref[:, at : at + wide] = halves_added(part)
    for copy in copies[len(first) :]:
        copy.wait()


def early(own, weights, places, pieces, width, after):
    rows2, depth = own.shape
    full = weights.shape[2]
    return call(
        functools.partial(early_kernel, pieces, width),
        "early_products",
        [places, own, weights],
        [
            jax.ShapeDtypeStruct((pieces * depth, full), jnp.bfloat16),
            jax.ShapeDtypeStruct((rows2 // 2, width), jnp.float32),
        ],
        after,
        [pltpu.SemaphoreType.DMA((len(spans(width, COLUMNS)) + pieces,))],
        limit=8,
        cost=(2 * rows2 * depth * width, 2 * pieces * depth * full, 0),
        far=1,
    )


def product_kernel(pieces, start, width, early, step, leave, stay, place_ref, near_ref, *refs):
    left = refs[:pieces]
    message_ref, kept_ref = refs[-2:]
    depth = left[0].shape[1]
    used = left[1:] if early else left
    low = depth if early else 0
    bounds = []
    for at, wide in spans(width, COLUMNS):
        columns = slice(start + at, start + at + wide)
        total = jnp.dot(
            jnp.concatenate([a_ref[...] for a_ref in used], axis=1),
            near_ref[low : pieces * depth, columns],
            preferred_element_type=jnp.float32,
        )
        total = halves_added(total)
        if early:
            total = total + refs[pieces][:, columns]
        for lane in range(0, wide, LANES):
            column = total[:, lane : lane + LANES]
            blocks = {p: column[p * step : (p + 1) * step] for p in leave + stay}
            tile = (at + lane) // LANES
            bounds.append(put_tile(message_ref, kept_ref, tile, blocks, step, leave, stay))
    put_bounds(message_ref, bounds, len(leave) * step)


def outputs(width, step, leave, stay):
    tiles = width // LANES
    sent = tiles * len(leave) * step + scale_rows(tiles)
    return [
        jax.ShapeDtypeStruct((sent, LANES), jnp.bfloat16),
        jax.ShapeDtypeStruct((tiles * len(stay) * step, LANES), jnp.float32),
    ]


def product(left, near, partial, places, start, width, step, leave, stay, after):
    rows2, depth = left[0].shape
    early = partial is not None
    count = len(left) - 1 if early else len(left)
    return call(
        functools.partial(
            product_kernel, len(left), start, width, early, step, leave, stay
        ),
        "product",
        [places, near, *left] + ([partial] if early else []),
        outputs(width, step, leave, stay),
        after,
        limit=8,
        cost=(
            2 * rows2 * depth * count * width,
            2 * depth * count * width + 4 * rows2 * width,
            rows2 * width // 4,
        ),
    )


def received(message_ref, kept_ref, tile, tiles, count):
    coded = message_ref[tile * count : (tile + 1) * count, :]
    group = tile // SCALE_ROWS * SCALE_ROWS
    at = tiles * count + group
    bounds = message_ref[at : at + SCALE_ROWS, :].astype(jnp.float32)
    bound = bounds[tile - group : tile - group + 1]
    return kept_ref[tile * count : (tile + 1) * count, :] + decode(coded, bound)


def middle_kernel(tiles, step, old, leave, stay, place_ref, message_ref, kept_ref, out_ref, next_ref):
    bounds = []
    for tile in range(tiles):
        column = received(message_ref, kept_ref, tile, tiles, len(old) * step)
        blocks = {p: column[i * step : (i + 1) * step] for i, p in enumerate(old)}
        bounds.append(put_tile(out_ref, next_ref, tile, blocks, step, leave, stay))
    put_bounds(out_ref, bounds, len(leave) * step)


def middle(message, kept, places, width, step, old, leave, stay, after):
    size = width * len(old) * step
    return call(
        functools.partial(middle_kernel, width // LANES, step, old, leave, stay),
        "add_and_split",
        [places, message, kept],
        outputs(width, step, leave, stay),
        after,
        cost=(20 * size, 9 * size, 2 * size),
    )


def last_kernel(tiles, pieces, place_ref, message_ref, kept_ref, *refs):
    outs = refs[:pieces]
    whole = refs[pieces]
    count = whole.shape[0]
    share = count // pieces
    for tile in range(tiles):
        whole[:, tile * LANES : (tile + 1) * LANES] = received(
            message_ref, kept_ref, tile, tiles, count
        )
    for distance in range(pieces):
        owner = jnp.bitwise_xor(place_ref[0], distance)
        rows = whole[pl.ds(pl.multiple_of(owner * share, share), share), :]
        outs[distance][...] = rows.astype(jnp.bfloat16)


def last(message, kept, places, width, step, pieces, after):
    size = width * step
    share = jax.ShapeDtypeStruct((step // pieces, width), jnp.bfloat16)
    return call(
        functools.partial(last_kernel, width // LANES, pieces),
        "add_last",
        [places, message, kept],
        [share] * pieces,
        after,
        [pltpu.VMEM((step, width), jnp.float32)],
        cost=(10 * size, 8 * size, size),
    )


def lay_kernel(pieces, width, place_ref, *refs):
    out_ref = refs[-1]
    at = 0
    for first in range(0, len(refs) - 1, pieces):
        for distance in range(pieces):
            part = refs[first + distance]
            owner = jnp.bitwise_xor(place_ref[0], distance)
            columns = pl.ds(pl.multiple_of(owner * width + at, LANES), part.shape[1])
            out_ref[:, columns] = part[...]
        at += part.shape[1]


def lay(parts, places, pieces, width):
    flat = [part for chunk in parts for part in chunk]
    rows = flat[0].shape[0]
    return call(
        functools.partial(lay_kernel, pieces, width),
        "lay_out",
        [places, *flat],
        [jax.ShapeDtypeStruct((rows, pieces * width), jnp.bfloat16)],
        [],
        cost=(0, 4 * rows * pieces * width, 0),
    )[0]


def swapped(block, apart):
    count = lax.axis_size("row")
    return lax.ppermute(block, "row", [(i, i ^ apart) for i in range(count)])


def on_device(basis, weights):
    axis_len = lax.axis_size("row")
    depth, rows = basis.shape
    pieces = weights.shape[1] // depth
    blocks = axis_len // pieces
    bits = blocks.bit_length() - 1
    piece_bits = pieces.bit_length() - 1
    step = rows // blocks
    width = weights.shape[2]
    me = lax.axis_index("row").astype(jnp.int32)
    column = jnp.bitwise_and(me, pieces - 1)
    places = jnp.stack([column, jnp.right_shift(me, piece_bits)])

    own = prepare(basis, places, blocks, bits)
    left = [own] + [swapped(own, distance) for distance in range(1, pieces)]

    cuts = [0]
    for share, _ in CHUNKS:
        cuts.append(cuts[-1] + share)
    cuts = [cut * (width // LANES) // PARTS * LANES for cut in cuts]
    orders = [[bit for bit in order if bit < bits] for _, order in CHUNKS]
    stages = [split_places(order, bits) for order in orders]
    near, partial = early(own, weights, places, pieces, cuts[EARLY], [])

    state = {}
    after = [partial]
    finished = {}
    for index, number in ORDER:
        order = orders[index]
        start = cuts[index]
        chunk = cuts[index + 1] - start
        if chunk == 0:
            continue
        if number == 0:
            begun = partial if index < EARLY else None
            out = product(
                left, near, begun, places, start, chunk, step, *stages[index][0], after
            )
        elif number < bits:
            message, kept = state[index]
            old = stages[index][number - 1][1]
            out = middle(message, kept, places, chunk, step, old, *stages[index][number], after)
        else:
            message, kept = state[index]
            out = last(message, kept, places, chunk, step, pieces, after)
            finished[index] = [out[0]] + [swapped(out[d], d) for d in range(1, pieces)]
            after = [out[0]]
            continue
        state[index] = swapped(out[0], pieces << order[number]), out[1]
        after = [out[1]]
    return lay([finished[index] for index in sorted(finished)], places, pieces, width)


def solution(mesh):
    in_specs = (P(("groups", "row"), None), P(("groups", "row"), None, None))
    out_specs = P(("groups", "row"), None)
    return jax.shard_map(
        on_device, mesh=mesh, in_specs=in_specs, out_specs=out_specs, check_vma=False
    )
```

```python
import functools

import jax
import jax.numpy as jnp
from jax import lax
from jax.experimental import pallas as pl
from jax.experimental.pallas import tpu as pltpu
from jax.sharding import PartitionSpec as P

LANES = 128
SCALE_ROWS = 16
COLUMNS = 256
HALF_SPAN = 125.0
SPAN = 250.0
TINY = 2.0**-110
MIB = 1 << 20

CHUNKS = [
    (3, (2, 0, 1)),
    (4, (0, 1, 2)),
    (3, (1, 0, 2)),
    (3, (0, 1, 2)),
    (3, (0, 1, 2)),
]
PARTS = 16
EARLY = 2
ORDER = [
    (0, 0), (1, 0), (2, 0), (3, 0), (1, 1), (4, 0), (3, 1), (1, 2),
    (2, 1), (4, 1), (3, 2), (0, 1), (2, 2), (4, 2), (0, 2), (3, 3),
    (2, 3), (1, 3), (4, 3), (0, 3),
]


def column_bound(values):
    top = jnp.maximum(jnp.max(jnp.abs(values), axis=0, keepdims=True), TINY)
    return (top * 1.008).astype(jnp.bfloat16).astype(jnp.float32)


def encode(values, bound):
    level = jnp.exp2(jnp.abs(values) * (SPAN / bound) - HALF_SPAN)
    return jnp.where(values < 0, -level, level).astype(jnp.bfloat16)


def decode(coded, bound):
    coded = coded.astype(jnp.float32)
    size = (jnp.log2(jnp.abs(coded)) + HALF_SPAN) * (bound * (1.0 / SPAN))
    return jnp.where(coded < 0, -size, size)


def reversed_bits(value, bits):
    out = 0
    for bit in range(bits):
        out |= (value >> bit & 1) << (bits - 1 - bit)
    return out


def split_places(order, bits):
    stay = list(range(1 << bits))
    stages = []
    for bit in order:
        leave = [p for p in stay if reversed_bits(p, bits) >> bit & 1]
        stay = [p for p in stay if not reversed_bits(p, bits) >> bit & 1]
        stages.append((leave, stay))
    return stages


def scale_rows(tiles):
    return -(-tiles // SCALE_ROWS) * SCALE_ROWS


def put_bounds(message_ref, bounds, count):
    tiles = len(bounds)
    spare = scale_rows(tiles) - tiles
    if spare:
        bounds = bounds + [jnp.zeros((spare, LANES), jnp.float32)]
    message_ref[tiles * count :, :] = jnp.concatenate(bounds, axis=0).astype(jnp.bfloat16)


def put_tile(message_ref, kept_ref, tile, blocks, step, leave, stay):
    sent = jnp.concatenate([blocks[p] for p in leave], axis=0)
    bound = column_bound(sent)
    count = len(leave) * step
    message_ref[tile * count : (tile + 1) * count, :] = encode(sent, bound)
    for slot, p in enumerate(stay):
        at = (tile * len(stay) + slot) * step
        kept_ref[at : at + step, :] = blocks[p]
    return bound


def call(kernel, name, ins, outs, after, scratch=(), limit=4, cost=(0, 0, 0), far=0):
    count = len(ins)

    def run(*refs):
        kernel(*refs[:count], *refs[count + len(after) :])

    vmem = pl.BlockSpec(memory_space=pltpu.VMEM)
    near = count - far
    ins = ins[:near] + [pltpu.with_memory_space_constraint(x, pltpu.HBM) for x in ins[near:]]
    return pl.pallas_call(
        run,
        in_specs=[pl.BlockSpec(memory_space=pltpu.SMEM)]
        + [vmem] * (count - 1 - far)
        + [pl.BlockSpec(memory_space=pltpu.HBM)] * far
        + [pl.BlockSpec(memory_space=pl.ANY)] * len(after),
        out_specs=[vmem] * len(outs),
        out_shape=outs,
        scratch_shapes=scratch,
        compiler_params=pltpu.CompilerParams(vmem_limit_bytes=limit * MIB),
        cost_estimate=pl.CostEstimate(
            flops=cost[0], bytes_accessed=cost[1], transcendentals=cost[2]
        ),
        name=name,
    )(*ins, *after)


def prepare_kernel(blocks, bits, wide, place_ref, basis_ref, out_ref, held, turned, sems):
    depth, rows = basis_ref.shape
    step = rows // blocks
    copies = []
    for index, at in enumerate(range(0, depth, wide)):
        part = pl.ds(at, wide)
        copies.append(
            pltpu.make_async_copy(basis_ref.at[part, :], held.at[part, :], sems.at[index])
        )
        copies[-1].start()
    for index, at in enumerate(range(0, depth, wide)):
        copies[index].wait()
        turned[:, at : at + wide] = held[at : at + wide, :].T
        for place in range(blocks):
            source = jnp.bitwise_xor(place_ref[1], reversed_bits(place, bits))
            part = turned[pl.ds(pl.multiple_of(source * step, step), step), at : at + wide]
            high = part.astype(jnp.bfloat16)
            low = (part - high.astype(jnp.float32)).astype(jnp.bfloat16)
            out_ref[place * step : (place + 1) * step, at : at + wide] = high
            out_ref[rows + place * step : rows + (place + 1) * step, at : at + wide] = low


def prepare(basis, places, blocks, bits):
    depth, rows = basis.shape
    wide = min(depth, COLUMNS)
    return call(
        functools.partial(prepare_kernel, blocks, bits, wide),
        "split_basis",
        [places, basis],
        [jax.ShapeDtypeStruct((2 * rows, depth), jnp.bfloat16)],
        [],
        [
            pltpu.VMEM((depth, rows), jnp.float32),
            pltpu.VMEM((rows, depth), jnp.float32),
            pltpu.SemaphoreType.DMA((depth // wide,)),
        ],
        limit=10,
        cost=(2 * depth * rows, 8 * depth * rows, 0),
        far=1,
    )[0]


def spans(width, wide):
    return [(at, min(wide, width - at)) for at in range(0, width, wide)]


def halves_added(product):
    half = product.shape[0] // 2
    return product[:half] + product[half:]


def weight_copies(place_ref, w_ref, near_ref, sems, start, depth, boxes):
    copies = []
    for index, (distance, row, rows, at, wide) in enumerate(boxes):
        owner = jnp.bitwise_xor(place_ref[0], distance)
        source = pl.ds(pl.multiple_of(owner * depth + row, rows), rows)
        target = pl.ds(distance * depth + row, rows)
        copies.append(
            pltpu.make_async_copy(
                w_ref.at[0, source, pl.ds(start + at, wide)],
                near_ref.at[target, pl.ds(at, wide)],
                sems.at[index],
            )
        )
    return copies


def row_boxes(distances, depth, width):
    return [
        (distance, row, rows, 0, width)
        for distance in distances
        for row, rows in spans(depth, COLUMNS)
    ]


def early_boxes(pieces, depth, width):
    first = [(0, 0, depth, at, wide) for at, wide in spans(width, 2 * COLUMNS)]
    return first, row_boxes(range(1, pieces), depth, width)


def early_kernel(pieces, width, place_ref, own_ref, w_ref, near_ref, partial_ref, sems):
    depth = own_ref.shape[1]
    first, rest = early_boxes(pieces, depth, width)
    copies = weight_copies(place_ref, w_ref, near_ref, sems, 0, depth, first + rest)
    for copy in copies:
        copy.start()
    for copy, (_, _, _, start, reach) in zip(copies, first):
        copy.wait()
        for at, wide in spans(reach, COLUMNS):
            columns = slice(start + at, start + at + wide)
            part = jnp.dot(
                own_ref[...], near_ref[0:depth, columns], preferred_element_type=jnp.float32
            )
            partial_ref[:, columns] = halves_added(part)
    for copy in copies[len(first) :]:
        copy.wait()


def early(own, weights, places, pieces, width, after):
    rows2, depth = own.shape
    first, rest = early_boxes(pieces, depth, width)
    return call(
        functools.partial(early_kernel, pieces, width),
        "early_products",
        [places, own, weights],
        [
            jax.ShapeDtypeStruct((pieces * depth, width), jnp.bfloat16),
            jax.ShapeDtypeStruct((rows2 // 2, width), jnp.float32),
        ],
        after,
        [pltpu.SemaphoreType.DMA((len(first) + len(rest),))],
        limit=8,
        cost=(2 * rows2 * depth * width, 2 * pieces * depth * width, 0),
        far=1,
    )


def product_kernel(pieces, start, width, early, bring, step, leave, stay, place_ref, near_ref, *refs):
    left = refs[:pieces]
    depth = left[0].shape[1]
    if bring:
        w_ref, message_ref, kept_ref, later_ref, sems = refs[-5:]
        boxes = row_boxes(range(pieces), depth, later_ref.shape[1])
        copies = weight_copies(place_ref, w_ref, later_ref, sems, bring, depth, boxes)
        for copy in copies:
            copy.start()
    else:
        message_ref, kept_ref = refs[-2:]
    used = left[1:] if early else left
    low = depth if early else 0
    bounds = []
    for at, wide in spans(width, COLUMNS):
        columns = slice(start + at, start + at + wide)
        total = jnp.dot(
            jnp.concatenate([a_ref[...] for a_ref in used], axis=1),
            near_ref[low : pieces * depth, columns],
            preferred_element_type=jnp.float32,
        )
        total = halves_added(total)
        if early:
            total = total + refs[pieces][:, columns]
        for lane in range(0, wide, LANES):
            column = total[:, lane : lane + LANES]
            blocks = {p: column[p * step : (p + 1) * step] for p in leave + stay}
            tile = (at + lane) // LANES
            bounds.append(put_tile(message_ref, kept_ref, tile, blocks, step, leave, stay))
    put_bounds(message_ref, bounds, len(leave) * step)
    if bring:
        for copy in copies:
            copy.wait()


def outputs(width, step, leave, stay):
    tiles = width // LANES
    sent = tiles * len(leave) * step + scale_rows(tiles)
    return [
        jax.ShapeDtypeStruct((sent, LANES), jnp.bfloat16),
        jax.ShapeDtypeStruct((tiles * len(stay) * step, LANES), jnp.float32),
    ]


def product(left, near, partial, weights, places, start, width, bring, step, leave, stay, after):
    rows2, depth = left[0].shape
    pieces = len(left)
    early = partial is not None
    count = pieces - 1 if early else pieces
    outs = outputs(width, step, leave, stay)
    scratch = []
    if bring:
        later = weights.shape[2] - bring
        outs.append(jax.ShapeDtypeStruct((pieces * depth, later), jnp.bfloat16))
        scratch = [pltpu.SemaphoreType.DMA((len(row_boxes(range(pieces), depth, later)),))]
    return call(
        functools.partial(
            product_kernel, pieces, start, width, early, bring, step, leave, stay
        ),
        "product",
        [places, near, *left] + ([partial] if early else []) + ([weights] if bring else []),
        outs,
        after,
        scratch,
        limit=8,
        cost=(
            2 * rows2 * depth * count * width,
            2 * depth * count * width + 4 * rows2 * width,
            rows2 * width // 4,
        ),
        far=1 if bring else 0,
    )


def received(message_ref, kept_ref, tile, tiles, count):
    coded = message_ref[tile * count : (tile + 1) * count, :]
    group = tile // SCALE_ROWS * SCALE_ROWS
    at = tiles * count + group
    bounds = message_ref[at : at + SCALE_ROWS, :].astype(jnp.float32)
    bound = bounds[tile - group : tile - group + 1]
    return kept_ref[tile * count : (tile + 1) * count, :] + decode(coded, bound)


def middle_kernel(tiles, step, old, leave, stay, place_ref, message_ref, kept_ref, out_ref, next_ref):
    bounds = []
    for tile in range(tiles):
        column = received(message_ref, kept_ref, tile, tiles, len(old) * step)
        blocks = {p: column[i * step : (i + 1) * step] for i, p in enumerate(old)}
        bounds.append(put_tile(out_ref, next_ref, tile, blocks, step, leave, stay))
    put_bounds(out_ref, bounds, len(leave) * step)


def middle(message, kept, places, width, step, old, leave, stay, after):
    size = width * len(old) * step
    return call(
        functools.partial(middle_kernel, width // LANES, step, old, leave, stay),
        "add_and_split",
        [places, message, kept],
        outputs(width, step, leave, stay),
        after,
        cost=(20 * size, 9 * size, 2 * size),
    )


def last_kernel(tiles, pieces, place_ref, message_ref, kept_ref, *refs):
    outs = refs[:pieces]
    whole = refs[pieces]
    count = whole.shape[0]
    share = count // pieces
    for tile in range(tiles):
        whole[:, tile * LANES : (tile + 1) * LANES] = received(
            message_ref, kept_ref, tile, tiles, count
        )
    for distance in range(pieces):
        owner = jnp.bitwise_xor(place_ref[0], distance)
        rows = whole[pl.ds(pl.multiple_of(owner * share, share), share), :]
        outs[distance][...] = rows.astype(jnp.bfloat16)


def last(message, kept, places, width, step, pieces, after):
    size = width * step
    share = jax.ShapeDtypeStruct((step // pieces, width), jnp.bfloat16)
    return call(
        functools.partial(last_kernel, width // LANES, pieces),
        "add_last",
        [places, message, kept],
        [share] * pieces,
        after,
        [pltpu.VMEM((step, width), jnp.float32)],
        cost=(10 * size, 8 * size, size),
    )


def lay_kernel(pieces, width, place_ref, *refs):
    out_ref = refs[-1]
    at = 0
    for first in range(0, len(refs) - 1, pieces):
        for distance in range(pieces):
            part = refs[first + distance]
            owner = jnp.bitwise_xor(place_ref[0], distance)
            columns = pl.ds(pl.multiple_of(owner * width + at, LANES), part.shape[1])
            out_ref[:, columns] = part[...]
        at += part.shape[1]


def lay(parts, places, pieces, width):
    flat = [part for chunk in parts for part in chunk]
    rows = flat[0].shape[0]
    return call(
        functools.partial(lay_kernel, pieces, width),
        "lay_out",
        [places, *flat],
        [jax.ShapeDtypeStruct((rows, pieces * width), jnp.bfloat16)],
        [],
        cost=(0, 4 * rows * pieces * width, 0),
    )[0]


def swapped(block, apart):
    count = lax.axis_size("row")
    return lax.ppermute(block, "row", [(i, i ^ apart) for i in range(count)])


def on_device(basis, weights):
    axis_len = lax.axis_size("row")
    depth, rows = basis.shape
    pieces = weights.shape[1] // depth
    blocks = axis_len // pieces
    bits = blocks.bit_length() - 1
    piece_bits = pieces.bit_length() - 1
    step = rows // blocks
    width = weights.shape[2]
    me = lax.axis_index("row").astype(jnp.int32)
    column = jnp.bitwise_and(me, pieces - 1)
    places = jnp.stack([column, jnp.right_shift(me, piece_bits)])

    own = prepare(basis, places, blocks, bits)
    left = [own] + [swapped(own, distance) for distance in range(1, pieces)]

    cuts = [0]
    for share, _ in CHUNKS:
        cuts.append(cuts[-1] + share)
    cuts = [cut * (width // LANES) // PARTS * LANES for cut in cuts]
    orders = [[bit for bit in order if bit < bits] for _, order in CHUNKS]
    stages = [split_places(order, bits) for order in orders]
    ahead = cuts[EARLY]
    near, partial = early(own, weights, places, pieces, ahead, [])

    state = {}
    after = [partial]
    finished = {}
    for index, number in ORDER:
        order = orders[index]
        start = cuts[index]
        chunk = cuts[index + 1] - start
        if chunk == 0:
            continue
        if number == 0:
            early_one = index < EARLY
            out = product(
                left,
                near if early_one else later,
                partial if early_one else None,
                weights,
                places,
                start if early_one else start - ahead,
                chunk,
                ahead if index == EARLY - 1 else 0,
                step,
                *stages[index][0],
                after,
            )
            if index == EARLY - 1:
                later = out[2]
        elif number < bits:
            message, kept = state[index]
            old = stages[index][number - 1][1]
            out = middle(message, kept, places, chunk, step, old, *stages[index][number], after)
        else:
            message, kept = state[index]
            out = last(message, kept, places, chunk, step, pieces, after)
            finished[index] = [out[0]] + [swapped(out[d], d) for d in range(1, pieces)]
            after = [out[0]]
            continue
        state[index] = swapped(out[0], pieces << order[number]), out[1]
        after = [out[1]]
    return lay([finished[index] for index in sorted(finished)], places, pieces, width)


def solution(mesh):
    in_specs = (P(("groups", "row"), None), P(("groups", "row"), None, None))
    out_specs = P(("groups", "row"), None)
    return jax.shard_map(
        on_device, mesh=mesh, in_specs=in_specs, out_specs=out_specs, check_vma=False
    )
```

```python
import functools

import jax
import jax.numpy as jnp
from jax import lax
from jax.experimental import pallas as pl
from jax.experimental.pallas import tpu as pltpu
from jax.sharding import PartitionSpec as P

LANES = 128
SCALE_ROWS = 16
COLUMNS = 256
HALF_SPAN = 125.0
SPAN = 250.0
TINY = 2.0**-110
MIB = 1 << 20

CHUNKS = [
    (3, (2, 0, 1)),
    (4, (1, 0, 2)),
    (3, (0, 2, 1)),
    (3, (0, 1, 2)),
    (3, (1, 0, 2)),
]
PARTS = 16
EARLY = 1
ORDER = [
    (0, 0), (1, 0), (2, 0), (3, 0), (4, 0), (1, 1), (2, 1), (3, 1),
    (0, 1), (4, 1), (1, 2), (2, 2), (4, 2), (0, 2), (3, 2), (1, 3),
    (2, 3), (0, 3), (4, 3), (3, 3),
]


def column_bound(values):
    top = jnp.maximum(jnp.max(jnp.abs(values), axis=0, keepdims=True), TINY)
    return (top * 1.008).astype(jnp.bfloat16).astype(jnp.float32)


def encode(values, bound):
    level = jnp.exp2(jnp.abs(values) * (SPAN / bound) - HALF_SPAN)
    return jnp.where(values < 0, -level, level).astype(jnp.bfloat16)


def decode(coded, bound):
    coded = coded.astype(jnp.float32)
    size = (jnp.log2(jnp.abs(coded)) + HALF_SPAN) * (bound * (1.0 / SPAN))
    return jnp.where(coded < 0, -size, size)


def reversed_bits(value, bits):
    out = 0
    for bit in range(bits):
        out |= (value >> bit & 1) << (bits - 1 - bit)
    return out


def split_places(order, bits):
    stay = list(range(1 << bits))
    stages = []
    for bit in order:
        leave = [p for p in stay if reversed_bits(p, bits) >> bit & 1]
        stay = [p for p in stay if not reversed_bits(p, bits) >> bit & 1]
        stages.append((leave, stay))
    return stages


def scale_rows(tiles):
    return -(-tiles // SCALE_ROWS) * SCALE_ROWS


def put_bounds(message_ref, bounds, count):
    tiles = len(bounds)
    spare = scale_rows(tiles) - tiles
    if spare:
        bounds = bounds + [jnp.zeros((spare, LANES), jnp.float32)]
    message_ref[tiles * count :, :] = jnp.concatenate(bounds, axis=0).astype(jnp.bfloat16)


def put_tile(message_ref, kept_ref, tile, blocks, step, leave, stay):
    sent = jnp.concatenate([blocks[p] for p in leave], axis=0)
    bound = column_bound(sent)
    count = len(leave) * step
    message_ref[tile * count : (tile + 1) * count, :] = encode(sent, bound)
    for slot, p in enumerate(stay):
        at = (tile * len(stay) + slot) * step
        kept_ref[at : at + step, :] = blocks[p]
    return bound


def call(kernel, name, ins, outs, after, scratch=(), limit=4, cost=(0, 0, 0), far=0):
    count = len(ins)

    def run(*refs):
        kernel(*refs[:count], *refs[count + len(after) :])

    vmem = pl.BlockSpec(memory_space=pltpu.VMEM)
    near = count - far
    ins = ins[:near] + [pltpu.with_memory_space_constraint(x, pltpu.HBM) for x in ins[near:]]
    return pl.pallas_call(
        run,
        in_specs=[pl.BlockSpec(memory_space=pltpu.SMEM)]
        + [vmem] * (count - 1 - far)
        + [pl.BlockSpec(memory_space=pltpu.HBM)] * far
        + [pl.BlockSpec(memory_space=pl.ANY)] * len(after),
        out_specs=[vmem] * len(outs),
        out_shape=outs,
        scratch_shapes=scratch,
        compiler_params=pltpu.CompilerParams(vmem_limit_bytes=limit * MIB),
        cost_estimate=pl.CostEstimate(
            flops=cost[0], bytes_accessed=cost[1], transcendentals=cost[2]
        ),
        name=name,
    )(*ins, *after)


def prepare_kernel(blocks, bits, wide, place_ref, basis_ref, out_ref, held, turned, sems):
    depth, rows = basis_ref.shape
    step = rows // blocks
    copies = []
    for index, at in enumerate(range(0, depth, wide)):
        part = pl.ds(at, wide)
        copies.append(
            pltpu.make_async_copy(basis_ref.at[part, :], held.at[part, :], sems.at[index])
        )
        copies[-1].start()
    for index, at in enumerate(range(0, depth, wide)):
        copies[index].wait()
        turned[:, at : at + wide] = held[at : at + wide, :].T
        for place in range(blocks):
            source = jnp.bitwise_xor(place_ref[1], reversed_bits(place, bits))
            part = turned[pl.ds(pl.multiple_of(source * step, step), step), at : at + wide]
            high = part.astype(jnp.bfloat16)
            low = (part - high.astype(jnp.float32)).astype(jnp.bfloat16)
            out_ref[place * step : (place + 1) * step, at : at + wide] = high
            out_ref[rows + place * step : rows + (place + 1) * step, at : at + wide] = low


def prepare(basis, places, blocks, bits):
    depth, rows = basis.shape
    wide = min(depth, COLUMNS)
    return call(
        functools.partial(prepare_kernel, blocks, bits, wide),
        "split_basis",
        [places, basis],
        [jax.ShapeDtypeStruct((2 * rows, depth), jnp.bfloat16)],
        [],
        [
            pltpu.VMEM((depth, rows), jnp.float32),
            pltpu.VMEM((rows, depth), jnp.float32),
            pltpu.SemaphoreType.DMA((depth // wide,)),
        ],
        limit=10,
        cost=(2 * depth * rows, 8 * depth * rows, 0),
        far=1,
    )[0]


def spans(width, wide):
    return [(at, min(wide, width - at)) for at in range(0, width, wide)]


def halves_added(product):
    half = product.shape[0] // 2
    return product[:half] + product[half:]


def weight_copies(place_ref, w_ref, near_ref, sems, start, depth, boxes):
    copies = []
    for index, (distance, row, rows, at, wide) in enumerate(boxes):
        owner = jnp.bitwise_xor(place_ref[0], distance)
        source = pl.ds(pl.multiple_of(owner * depth + row, rows), rows)
        target = pl.ds(distance * depth + row, rows)
        copies.append(
            pltpu.make_async_copy(
                w_ref.at[0, source, pl.ds(start + at, wide)],
                near_ref.at[target, pl.ds(at, wide)],
                sems.at[index],
            )
        )
    return copies


def row_boxes(distances, depth, width):
    return [
        (distance, row, rows, 0, width)
        for distance in distances
        for row, rows in spans(depth, COLUMNS)
    ]


def early_boxes(pieces, depth, width):
    first = [(0, 0, depth, at, wide) for at, wide in spans(width, 2 * COLUMNS)]
    return first, row_boxes(range(1, pieces), depth, width)


def early_kernel(pieces, width, place_ref, own_ref, w_ref, near_ref, partial_ref, sems):
    depth = own_ref.shape[1]
    first, rest = early_boxes(pieces, depth, width)
    copies = weight_copies(place_ref, w_ref, near_ref, sems, 0, depth, first + rest)
    for copy in copies:
        copy.start()
    for copy, (_, _, _, start, reach) in zip(copies, first):
        copy.wait()
        for at, wide in spans(reach, COLUMNS):
            columns = slice(start + at, start + at + wide)
            part = jnp.dot(
                own_ref[...], near_ref[0:depth, columns], preferred_element_type=jnp.float32
            )
            partial_ref[:, columns] = halves_added(part)
    for copy in copies[len(first) :]:
        copy.wait()


def early(own, weights, places, pieces, width, after):
    rows2, depth = own.shape
    first, rest = early_boxes(pieces, depth, width)
    return call(
        functools.partial(early_kernel, pieces, width),
        "early_products",
        [places, own, weights],
        [
            jax.ShapeDtypeStruct((pieces * depth, width), jnp.bfloat16),
            jax.ShapeDtypeStruct((rows2 // 2, width), jnp.float32),
        ],
        after,
        [pltpu.SemaphoreType.DMA((len(first) + len(rest),))],
        limit=8,
        cost=(2 * rows2 * depth * width, 2 * pieces * depth * width, 0),
        far=1,
    )


def product_kernel(pieces, start, width, early, bring, step, leave, stay, place_ref, near_ref, *refs):
    left = refs[:pieces]
    depth = left[0].shape[1]
    if bring:
        w_ref, message_ref, kept_ref, later_ref, sems = refs[-5:]
        boxes = row_boxes(range(pieces), depth, later_ref.shape[1])
        copies = weight_copies(place_ref, w_ref, later_ref, sems, bring.start, depth, boxes)
        for copy in copies:
            copy.start()
    else:
        message_ref, kept_ref = refs[-2:]
    used = left[1:] if early else left
    low = depth if early else 0
    bounds = []
    for at, wide in spans(width, COLUMNS):
        columns = slice(start + at, start + at + wide)
        total = jnp.dot(
            jnp.concatenate([a_ref[...] for a_ref in used], axis=1),
            near_ref[low : pieces * depth, columns],
            preferred_element_type=jnp.float32,
        )
        total = halves_added(total)
        if early:
            total = total + refs[pieces][:, columns]
        for lane in range(0, wide, LANES):
            column = total[:, lane : lane + LANES]
            blocks = {p: column[p * step : (p + 1) * step] for p in leave + stay}
            tile = (at + lane) // LANES
            bounds.append(put_tile(message_ref, kept_ref, tile, blocks, step, leave, stay))
    put_bounds(message_ref, bounds, len(leave) * step)
    if bring:
        for copy in copies:
            copy.wait()


def outputs(width, step, leave, stay):
    tiles = width // LANES
    sent = tiles * len(leave) * step + scale_rows(tiles)
    return [
        jax.ShapeDtypeStruct((sent, LANES), jnp.bfloat16),
        jax.ShapeDtypeStruct((tiles * len(stay) * step, LANES), jnp.float32),
    ]


def product(left, near, partial, weights, places, start, width, bring, step, leave, stay, after):
    rows2, depth = left[0].shape
    pieces = len(left)
    early = partial is not None
    count = pieces - 1 if early else pieces
    outs = outputs(width, step, leave, stay)
    scratch = []
    if bring:
        later = bring.stop - bring.start
        outs.append(jax.ShapeDtypeStruct((pieces * depth, later), jnp.bfloat16))
        scratch = [pltpu.SemaphoreType.DMA((len(row_boxes(range(pieces), depth, later)),))]
    return call(
        functools.partial(
            product_kernel, pieces, start, width, early, bring, step, leave, stay
        ),
        "product",
        [places, near, *left] + ([partial] if early else []) + ([weights] if bring else []),
        outs,
        after,
        scratch,
        limit=8,
        cost=(
            2 * rows2 * depth * count * width,
            2 * depth * count * width + 4 * rows2 * width,
            rows2 * width // 4,
        ),
        far=1 if bring else 0,
    )


def received(message_ref, kept_ref, tile, tiles, count):
    coded = message_ref[tile * count : (tile + 1) * count, :]
    group = tile // SCALE_ROWS * SCALE_ROWS
    at = tiles * count + group
    bounds = message_ref[at : at + SCALE_ROWS, :].astype(jnp.float32)
    bound = bounds[tile - group : tile - group + 1]
    return kept_ref[tile * count : (tile + 1) * count, :] + decode(coded, bound)


def middle_kernel(tiles, step, old, leave, stay, place_ref, message_ref, kept_ref, out_ref, next_ref):
    bounds = []
    for tile in range(tiles):
        column = received(message_ref, kept_ref, tile, tiles, len(old) * step)
        blocks = {p: column[i * step : (i + 1) * step] for i, p in enumerate(old)}
        bounds.append(put_tile(out_ref, next_ref, tile, blocks, step, leave, stay))
    put_bounds(out_ref, bounds, len(leave) * step)


def middle(message, kept, places, width, step, old, leave, stay, after):
    size = width * len(old) * step
    return call(
        functools.partial(middle_kernel, width // LANES, step, old, leave, stay),
        "add_and_split",
        [places, message, kept],
        outputs(width, step, leave, stay),
        after,
        cost=(20 * size, 9 * size, 2 * size),
    )


def last_kernel(tiles, pieces, place_ref, message_ref, kept_ref, *refs):
    outs = refs[:pieces]
    whole = refs[pieces]
    count = whole.shape[0]
    share = count // pieces
    for tile in range(tiles):
        whole[:, tile * LANES : (tile + 1) * LANES] = received(
            message_ref, kept_ref, tile, tiles, count
        )
    for distance in range(pieces):
        owner = jnp.bitwise_xor(place_ref[0], distance)
        rows = whole[pl.ds(pl.multiple_of(owner * share, share), share), :]
        outs[distance][...] = rows.astype(jnp.bfloat16)


def last(message, kept, places, width, step, pieces, after):
    size = width * step
    share = jax.ShapeDtypeStruct((step // pieces, width), jnp.bfloat16)
    return call(
        functools.partial(last_kernel, width // LANES, pieces),
        "add_last",
        [places, message, kept],
        [share] * pieces,
        after,
        [pltpu.VMEM((step, width), jnp.float32)],
        cost=(10 * size, 8 * size, size),
    )


def lay_kernel(pieces, width, place_ref, *refs):
    out_ref = refs[-1]
    at = 0
    for first in range(0, len(refs) - 1, pieces):
        for distance in range(pieces):
            part = refs[first + distance]
            owner = jnp.bitwise_xor(place_ref[0], distance)
            columns = pl.ds(pl.multiple_of(owner * width + at, LANES), part.shape[1])
            out_ref[:, columns] = part[...]
        at += part.shape[1]


def lay(parts, places, pieces, width):
    flat = [part for chunk in parts for part in chunk]
    rows = flat[0].shape[0]
    return call(
        functools.partial(lay_kernel, pieces, width),
        "lay_out",
        [places, *flat],
        [jax.ShapeDtypeStruct((rows, pieces * width), jnp.bfloat16)],
        [],
        cost=(0, 4 * rows * pieces * width, 0),
    )[0]


def swapped(block, apart):
    count = lax.axis_size("row")
    return lax.ppermute(block, "row", [(i, i ^ apart) for i in range(count)])


def on_device(basis, weights):
    axis_len = lax.axis_size("row")
    depth, rows = basis.shape
    pieces = weights.shape[1] // depth
    blocks = axis_len // pieces
    bits = blocks.bit_length() - 1
    piece_bits = pieces.bit_length() - 1
    step = rows // blocks
    width = weights.shape[2]
    me = lax.axis_index("row").astype(jnp.int32)
    column = jnp.bitwise_and(me, pieces - 1)
    places = jnp.stack([column, jnp.right_shift(me, piece_bits)])

    own = prepare(basis, places, blocks, bits)
    left = [own] + [swapped(own, distance) for distance in range(1, pieces)]

    cuts = [0]
    for share, _ in CHUNKS:
        cuts.append(cuts[-1] + share)
    cuts = [cut * (width // LANES) // PARTS * LANES for cut in cuts]
    orders = [[bit for bit in order if bit < bits] for _, order in CHUNKS]
    stages = [split_places(order, bits) for order in orders]
    near, partial = early(own, weights, places, pieces, cuts[EARLY], [])

    held = {}
    state = {}
    after = [partial]
    finished = {}
    for index, number in ORDER:
        order = orders[index]
        start = cuts[index]
        chunk = cuts[index + 1] - start
        if number == 0:
            early_one = index < EARLY
            ahead = index + EARLY
            bring = slice(*cuts[ahead : ahead + 2]) if ahead < len(CHUNKS) else None
            out = product(
                left,
                near if early_one else held[index],
                partial if early_one else None,
                weights,
                places,
                start if early_one else 0,
                chunk,
                bring,
                step,
                *stages[index][0],
                after,
            )
            if bring:
                held[ahead] = out[2]
        elif number < bits:
            message, kept = state[index]
            old = stages[index][number - 1][1]
            out = middle(message, kept, places, chunk, step, old, *stages[index][number], after)
        else:
            message, kept = state[index]
            out = last(message, kept, places, chunk, step, pieces, after)
            finished[index] = [out[0]] + [swapped(out[d], d) for d in range(1, pieces)]
            after = [out[0]]
            continue
        state[index] = swapped(out[0], pieces << order[number]), out[1]
        after = [out[1]]
    return lay([finished[index] for index in sorted(finished)], places, pieces, width)


def solution(mesh):
    in_specs = (P(("groups", "row"), None), P(("groups", "row"), None, None))
    out_specs = P(("groups", "row"), None)
    return jax.shard_map(
        on_device, mesh=mesh, in_specs=in_specs, out_specs=out_specs, check_vma=False
    )
```

```python
import functools

import jax
import jax.numpy as jnp
from jax import lax
from jax.experimental import pallas as pl
from jax.experimental.pallas import tpu as pltpu
from jax.sharding import PartitionSpec as P

LANES = 128
SCALE_ROWS = 16
COLUMNS = 256
HALF_SPAN = 125.0
SPAN = 250.0
TINY = 2.0**-110
MIB = 1 << 20

CHUNKS = [
    (4, (0, 2, 1)),
    (4, (1, 0, 2)),
    (4, (0, 2, 1)),
    (2, (1, 0, 2)),
    (2, (0, 1, 2)),
]
PARTS = 16
EARLY = 1
ORDER = [
    (0, 0), (1, 0), (2, 0), (0, 1), (3, 0), (4, 0), (1, 1), (2, 1),
    (0, 2), (3, 1), (4, 1), (1, 2), (2, 2), (0, 3), (3, 2), (4, 2),
    (1, 3), (2, 3), (3, 3), (4, 3),
]


def column_bound(values):
    top = jnp.maximum(jnp.max(jnp.abs(values), axis=0, keepdims=True), TINY)
    return (top * 1.008).astype(jnp.bfloat16).astype(jnp.float32)


def encode(values, bound):
    level = jnp.exp2(jnp.abs(values) * (SPAN / bound) - HALF_SPAN)
    return jnp.where(values < 0, -level, level).astype(jnp.bfloat16)


def decode(coded, bound):
    coded = coded.astype(jnp.float32)
    size = (jnp.log2(jnp.abs(coded)) + HALF_SPAN) * (bound * (1.0 / SPAN))
    return jnp.where(coded < 0, -size, size)


def reversed_bits(value, bits):
    out = 0
    for bit in range(bits):
        out |= (value >> bit & 1) << (bits - 1 - bit)
    return out


def split_places(order, bits):
    stay = list(range(1 << bits))
    stages = []
    for bit in order:
        leave = [p for p in stay if reversed_bits(p, bits) >> bit & 1]
        stay = [p for p in stay if not reversed_bits(p, bits) >> bit & 1]
        stages.append((leave, stay))
    return stages


def scale_rows(tiles):
    return -(-tiles // SCALE_ROWS) * SCALE_ROWS


def put_bounds(message_ref, bounds, count):
    tiles = len(bounds)
    spare = scale_rows(tiles) - tiles
    if spare:
        bounds = bounds + [jnp.zeros((spare, LANES), jnp.float32)]
    message_ref[tiles * count :, :] = jnp.concatenate(bounds, axis=0).astype(jnp.bfloat16)


def put_tile(message_ref, kept_ref, tile, blocks, step, leave, stay):
    sent = jnp.concatenate([blocks[p] for p in leave], axis=0)
    bound = column_bound(sent)
    count = len(leave) * step
    message_ref[tile * count : (tile + 1) * count, :] = encode(sent, bound)
    for slot, p in enumerate(stay):
        at = (tile * len(stay) + slot) * step
        kept_ref[at : at + step, :] = blocks[p]
    return bound


def call(kernel, name, ins, outs, after, scratch=(), limit=4, cost=(0, 0, 0), far=0):
    count = len(ins)

    def run(*refs):
        kernel(*refs[:count], *refs[count + len(after) :])

    vmem = pl.BlockSpec(memory_space=pltpu.VMEM)
    near = count - far
    ins = ins[:near] + [pltpu.with_memory_space_constraint(x, pltpu.HBM) for x in ins[near:]]
    return pl.pallas_call(
        run,
        in_specs=[pl.BlockSpec(memory_space=pltpu.SMEM)]
        + [vmem] * (count - 1 - far)
        + [pl.BlockSpec(memory_space=pltpu.HBM)] * far
        + [pl.BlockSpec(memory_space=pl.ANY)] * len(after),
        out_specs=[vmem] * len(outs),
        out_shape=outs,
        scratch_shapes=scratch,
        compiler_params=pltpu.CompilerParams(vmem_limit_bytes=limit * MIB),
        cost_estimate=pl.CostEstimate(flops=1, bytes_accessed=1, transcendentals=0),
        name=name,
    )(*ins, *after)


def row_copies(place_ref, w_ref, near_ref, sems, distance, wide):
    depth = near_ref.shape[0]
    owner = jnp.bitwise_xor(place_ref[0], distance)
    copies = []
    for index, at in enumerate(range(0, depth, wide)):
        source = pl.ds(pl.multiple_of(owner * depth + at, wide), wide)
        copies.append(
            pltpu.make_async_copy(
                w_ref.at[0, source, :], near_ref.at[pl.ds(at, wide), :], sems.at[index]
            )
        )
    return copies


def prepare_kernel(
    blocks, bits, wide, place_ref, basis_ref, w_ref, out_ref, near_ref, held, turned, sems, w_sems
):
    depth, rows = basis_ref.shape
    step = rows // blocks
    copies = []
    for index, at in enumerate(range(0, depth, wide)):
        part = pl.ds(at, wide)
        copies.append(
            pltpu.make_async_copy(basis_ref.at[part, :], held.at[part, :], sems.at[index])
        )
    weight_copies = row_copies(place_ref, w_ref, near_ref, w_sems, 0, wide)
    for copy in copies + weight_copies:
        copy.start()
    for index, at in enumerate(range(0, depth, wide)):
        copies[index].wait()
        turned[:, at : at + wide] = held[at : at + wide, :].T
        for place in range(blocks):
            source = jnp.bitwise_xor(place_ref[1], reversed_bits(place, bits))
            part = turned[pl.ds(pl.multiple_of(source * step, step), step), at : at + wide]
            high = part.astype(jnp.bfloat16)
            low = (part - high.astype(jnp.float32)).astype(jnp.bfloat16)
            out_ref[place * step : (place + 1) * step, at : at + wide] = high
            out_ref[rows + place * step : rows + (place + 1) * step, at : at + wide] = low
    for copy in weight_copies:
        copy.wait()


def prepare(basis, weights, places, blocks, bits):
    depth, rows = basis.shape
    wide = min(depth, COLUMNS)
    sems = pltpu.SemaphoreType.DMA((depth // wide,))
    return call(
        functools.partial(prepare_kernel, blocks, bits, wide),
        "split_basis",
        [places, basis, weights],
        [
            jax.ShapeDtypeStruct((2 * rows, depth), jnp.bfloat16),
            jax.ShapeDtypeStruct((depth, weights.shape[2]), jnp.bfloat16),
        ],
        [],
        [
            pltpu.VMEM((depth, rows), jnp.float32),
            pltpu.VMEM((rows, depth), jnp.float32),
            sems,
            sems,
        ],
        limit=10,
        cost=(2 * depth * rows, 8 * depth * rows, 0),
        far=2,
    )


def spans(width, wide):
    return [(at, min(wide, width - at)) for at in range(0, width, wide)]


def halves_added(product):
    half = product.shape[0] // 2
    return product[:half] + product[half:]


def early_kernel(pieces, width, place_ref, own_ref, near_ref, w_ref, *refs):
    *other_refs, partial_ref, sems = refs
    depth = own_ref.shape[1]
    wide = min(depth, COLUMNS)
    copies = []
    for distance in range(1, pieces):
        copies += row_copies(
            place_ref, w_ref, other_refs[distance - 1], sems.at[distance - 1], distance, wide
        )
    for copy in copies:
        copy.start()
    for at, wide in spans(width, COLUMNS):
        columns = slice(at, at + wide)
        part = jnp.dot(own_ref[...], near_ref[:, columns], preferred_element_type=jnp.float32)
        partial_ref[:, columns] = halves_added(part)
    for copy in copies:
        copy.wait()


def early(own, near, weights, places, pieces, width):
    rows2, depth = own.shape
    full = weights.shape[2]
    out = call(
        functools.partial(early_kernel, pieces, width),
        "early_products",
        [places, own, near, weights],
        [jax.ShapeDtypeStruct((depth, full), jnp.bfloat16)] * (pieces - 1)
        + [jax.ShapeDtypeStruct((rows2 // 2, width), jnp.float32)],
        [],
        [pltpu.SemaphoreType.DMA((pieces - 1, depth // min(depth, COLUMNS)))],
        limit=8,
        cost=(2 * rows2 * depth * width, 2 * pieces * depth * full, 0),
        far=1,
    )
    return [near, *out[:-1]], out[-1]


def product_kernel(pieces, start, width, early, step, leave, stay, place_ref, *refs):
    left, right = refs[:pieces], refs[pieces : 2 * pieces]
    message_ref, kept_ref = refs[-2:]
    first = 1 if early else 0
    bounds = []
    for at, wide in spans(width, COLUMNS):
        columns = slice(start + at, start + at + wide)
        total = jnp.dot(
            jnp.concatenate([a_ref[...] for a_ref in left[first:]], axis=1),
            jnp.concatenate([w_ref[:, columns] for w_ref in right[first:]], axis=0),
            preferred_element_type=jnp.float32,
        )
        total = halves_added(total)
        if early:
            total = total + refs[2 * pieces][:, columns]
        for lane in range(0, wide, LANES):
            column = total[:, lane : lane + LANES]
            blocks = {p: column[p * step : (p + 1) * step] for p in leave + stay}
            tile = (at + lane) // LANES
            bounds.append(put_tile(message_ref, kept_ref, tile, blocks, step, leave, stay))
    put_bounds(message_ref, bounds, len(leave) * step)


def outputs(width, step, leave, stay):
    tiles = width // LANES
    sent = tiles * len(leave) * step + scale_rows(tiles)
    return [
        jax.ShapeDtypeStruct((sent, LANES), jnp.bfloat16),
        jax.ShapeDtypeStruct((tiles * len(stay) * step, LANES), jnp.float32),
    ]


def product(left, right, partial, places, start, width, step, leave, stay, after):
    rows2, depth = left[0].shape
    pieces = len(left)
    early = partial is not None
    count = pieces - 1 if early else pieces
    return call(
        functools.partial(product_kernel, pieces, start, width, early, step, leave, stay),
        "product",
        [places, *left, *right] + ([partial] if early else []),
        outputs(width, step, leave, stay),
        after,
        limit=8,
        cost=(
            2 * rows2 * depth * count * width,
            2 * depth * count * width + 4 * rows2 * width,
            rows2 * width // 4,
        ),
    )


def received(message_ref, kept_ref, tile, tiles, count):
    coded = message_ref[tile * count : (tile + 1) * count, :]
    group = tile // SCALE_ROWS * SCALE_ROWS
    at = tiles * count + group
    bounds = message_ref[at : at + SCALE_ROWS, :].astype(jnp.float32)
    bound = bounds[tile - group : tile - group + 1]
    return kept_ref[tile * count : (tile + 1) * count, :] + decode(coded, bound)


def middle_kernel(tiles, step, old, leave, stay, place_ref, message_ref, kept_ref, out_ref, next_ref):
    bounds = []
    for tile in range(tiles):
        column = received(message_ref, kept_ref, tile, tiles, len(old) * step)
        blocks = {p: column[i * step : (i + 1) * step] for i, p in enumerate(old)}
        bounds.append(put_tile(out_ref, next_ref, tile, blocks, step, leave, stay))
    put_bounds(out_ref, bounds, len(leave) * step)


def middle(message, kept, places, width, step, old, leave, stay, after):
    size = width * len(old) * step
    return call(
        functools.partial(middle_kernel, width // LANES, step, old, leave, stay),
        "add_and_split",
        [places, message, kept],
        outputs(width, step, leave, stay),
        after,
        cost=(20 * size, 9 * size, 2 * size),
    )


def last_kernel(tiles, pieces, place_ref, message_ref, kept_ref, *refs):
    outs = refs[:pieces]
    whole = refs[pieces]
    count = whole.shape[0]
    share = count // pieces
    for tile in range(tiles):
        whole[:, tile * LANES : (tile + 1) * LANES] = received(
            message_ref, kept_ref, tile, tiles, count
        )
    for distance in range(pieces):
        owner = jnp.bitwise_xor(place_ref[0], distance)
        rows = whole[pl.ds(pl.multiple_of(owner * share, share), share), :]
        outs[distance][...] = rows.astype(jnp.bfloat16)


def last(message, kept, places, width, step, pieces, after):
    size = width * step
    share = jax.ShapeDtypeStruct((step // pieces, width), jnp.bfloat16)
    return call(
        functools.partial(last_kernel, width // LANES, pieces),
        "add_last",
        [places, message, kept],
        [share] * pieces,
        after,
        [pltpu.VMEM((step, width), jnp.float32)],
        cost=(10 * size, 8 * size, size),
    )


def lay_kernel(pieces, width, place_ref, *refs):
    out_ref = refs[-1]
    at = 0
    for first in range(0, len(refs) - 1, pieces):
        for distance in range(pieces):
            part = refs[first + distance]
            owner = jnp.bitwise_xor(place_ref[0], distance)
            columns = pl.ds(pl.multiple_of(owner * width + at, LANES), part.shape[1])
            out_ref[:, columns] = part[...]
        at += part.shape[1]


def lay(parts, places, pieces, width):
    flat = [part for chunk in parts for part in chunk]
    rows = flat[0].shape[0]
    return call(
        functools.partial(lay_kernel, pieces, width),
        "lay_out",
        [places, *flat],
        [jax.ShapeDtypeStruct((rows, pieces * width), jnp.bfloat16)],
        [],
        cost=(0, 4 * rows * pieces * width, 0),
    )[0]


def swapped(block, apart):
    count = lax.axis_size("row")
    return lax.ppermute(block, "row", [(i, i ^ apart) for i in range(count)])


def on_device(basis, weights):
    axis_len = lax.axis_size("row")
    depth, rows = basis.shape
    pieces = weights.shape[1] // depth
    blocks = axis_len // pieces
    bits = blocks.bit_length() - 1
    piece_bits = pieces.bit_length() - 1
    step = rows // blocks
    width = weights.shape[2]
    me = lax.axis_index("row").astype(jnp.int32)
    column = jnp.bitwise_and(me, pieces - 1)
    places = jnp.stack([column, jnp.right_shift(me, piece_bits)])

    own, near = prepare(basis, weights, places, blocks, bits)
    left = [own] + [swapped(own, distance) for distance in range(1, pieces)]

    cuts = [0]
    for share, _ in CHUNKS:
        cuts.append(cuts[-1] + share)
    cuts = [cut * (width // LANES) // PARTS * LANES for cut in cuts]
    orders = [[bit for bit in order if bit < bits] for _, order in CHUNKS]
    stages = [split_places(order, bits) for order in orders]
    right, partial = early(own, near, weights, places, pieces, cuts[EARLY])

    state = {}
    after = [partial]
    finished = {}
    for index, number in ORDER:
        order = orders[index]
        start = cuts[index]
        chunk = cuts[index + 1] - start
        if number == 0:
            begun = partial if index < EARLY else None
            out = product(
                left, right, begun, places, start, chunk, step, *stages[index][0], after
            )
        elif number < bits:
            message, kept = state[index]
            old = stages[index][number - 1][1]
            out = middle(message, kept, places, chunk, step, old, *stages[index][number], after)
        else:
            message, kept = state[index]
            out = last(message, kept, places, chunk, step, pieces, after)
            finished[index] = [out[0]] + [swapped(out[d], d) for d in range(1, pieces)]
            after = [out[0]]
            continue
        state[index] = swapped(out[0], pieces << order[number]), out[1]
        after = [out[1]]
    return lay([finished[index] for index in sorted(finished)], places, pieces, width)


def solution(mesh):
    in_specs = (P(("groups", "row"), None), P(("groups", "row"), None, None))
    out_specs = P(("groups", "row"), None)
    return jax.shard_map(
        on_device, mesh=mesh, in_specs=in_specs, out_specs=out_specs, check_vma=False
    )
```

```python
import functools

import jax
import jax.numpy as jnp
from jax import lax
from jax.experimental import pallas as pl
from jax.experimental.pallas import tpu as pltpu
from jax.sharding import PartitionSpec as P

LANES = 128
SCALE_ROWS = 16
COLUMNS = 256
HALF_SPAN = 125.0
SPAN = 250.0
TINY = 2.0**-110
MIB = 1 << 20

CHUNKS = [
    (4, (0, 2, 1)),
    (4, (1, 0, 2)),
    (4, (0, 2, 1)),
    (2, (1, 0, 2)),
    (2, (0, 1, 2)),
]
PARTS = 16
EARLY = 2
ORDER = [
    (0, 0), (1, 0), (2, 0), (0, 1), (3, 0), (4, 0), (1, 1), (2, 1),
    (0, 2), (3, 1), (4, 1), (1, 2), (2, 2), (0, 3), (3, 2), (4, 2),
    (1, 3), (2, 3), (3, 3), (4, 3),
]


def column_bound(values):
    top = jnp.maximum(jnp.max(jnp.abs(values), axis=0, keepdims=True), TINY)
    return (top * 1.008).astype(jnp.bfloat16).astype(jnp.float32)


def encode(values, bound):
    level = jnp.exp2(jnp.abs(values) * (SPAN / bound) - HALF_SPAN)
    return jnp.where(values < 0, -level, level).astype(jnp.bfloat16)


def decode(coded, bound):
    coded = coded.astype(jnp.float32)
    size = (jnp.log2(jnp.abs(coded)) + HALF_SPAN) * (bound * (1.0 / SPAN))
    return jnp.where(coded < 0, -size, size)


def reversed_bits(value, bits):
    out = 0
    for bit in range(bits):
        out |= (value >> bit & 1) << (bits - 1 - bit)
    return out


def split_places(order, bits):
    stay = list(range(1 << bits))
    stages = []
    for bit in order:
        leave = [p for p in stay if reversed_bits(p, bits) >> bit & 1]
        stay = [p for p in stay if not reversed_bits(p, bits) >> bit & 1]
        stages.append((leave, stay))
    return stages


def scale_rows(tiles):
    return -(-tiles // SCALE_ROWS) * SCALE_ROWS


def put_bounds(message_ref, bounds, count):
    tiles = len(bounds)
    spare = scale_rows(tiles) - tiles
    if spare:
        bounds = bounds + [jnp.zeros((spare, LANES), jnp.float32)]
    message_ref[tiles * count :, :] = jnp.concatenate(bounds, axis=0).astype(jnp.bfloat16)


def put_tile(message_ref, kept_ref, tile, blocks, step, leave, stay):
    sent = jnp.concatenate([blocks[p] for p in leave], axis=0)
    bound = column_bound(sent)
    count = len(leave) * step
    message_ref[tile * count : (tile + 1) * count, :] = encode(sent, bound)
    for slot, p in enumerate(stay):
        at = (tile * len(stay) + slot) * step
        kept_ref[at : at + step, :] = blocks[p]
    return bound


def position(pieces):
    me = lax.axis_index("row").astype(jnp.int32)
    return jnp.bitwise_and(me, pieces - 1), jnp.right_shift(me, pieces.bit_length() - 1)


def call(kernel, name, ins, outs, after, scratch=(), limit=4, cost=(0, 0, 0), far=0):
    count = len(ins)

    def run(*refs):
        kernel(*refs[:count], *refs[count + len(after) :])

    vmem = pl.BlockSpec(memory_space=pltpu.VMEM)
    near = count - far
    ins = ins[:near] + [pltpu.with_memory_space_constraint(x, pltpu.HBM) for x in ins[near:]]
    return pl.pallas_call(
        run,
        in_specs=[vmem] * (count - far)
        + [pl.BlockSpec(memory_space=pltpu.HBM)] * far
        + [pl.BlockSpec(memory_space=pl.ANY)] * len(after),
        out_specs=[vmem] * len(outs),
        out_shape=outs,
        scratch_shapes=scratch,
        compiler_params=pltpu.CompilerParams(vmem_limit_bytes=limit * MIB),
        cost_estimate=pl.CostEstimate(flops=1, bytes_accessed=1, transcendentals=0),
        name=name,
    )(*ins, *after)


def row_copies(w_ref, near_ref, sems, pieces, distance, wide):
    depth = near_ref.shape[0]
    owner = jnp.bitwise_xor(position(pieces)[0], distance)
    copies = []
    for index, at in enumerate(range(0, depth, wide)):
        source = pl.ds(pl.multiple_of(owner * depth + at, wide), wide)
        copies.append(
            pltpu.make_async_copy(
                w_ref.at[0, source, :], near_ref.at[pl.ds(at, wide), :], sems.at[index]
            )
        )
    return copies


def prepare_kernel(
    pieces, blocks, bits, wide, basis_ref, w_ref, out_ref, near_ref, held, turned, sems, w_sems
):
    depth, rows = basis_ref.shape
    step = rows // blocks
    mine = position(pieces)[1]
    copies = []
    for index, at in enumerate(range(0, depth, wide)):
        part = pl.ds(at, wide)
        copies.append(
            pltpu.make_async_copy(basis_ref.at[part, :], held.at[part, :], sems.at[index])
        )
    weight_copies = row_copies(w_ref, near_ref, w_sems, pieces, 0, wide)
    for copy in copies + weight_copies:
        copy.start()
    for index, at in enumerate(range(0, depth, wide)):
        copies[index].wait()
        turned[:, at : at + wide] = held[at : at + wide, :].T
        for place in range(blocks):
            source = jnp.bitwise_xor(mine, reversed_bits(place, bits))
            part = turned[pl.ds(pl.multiple_of(source * step, step), step), at : at + wide]
            high = part.astype(jnp.bfloat16)
            low = (part - high.astype(jnp.float32)).astype(jnp.bfloat16)
            out_ref[place * step : (place + 1) * step, at : at + wide] = high
            out_ref[rows + place * step : rows + (place + 1) * step, at : at + wide] = low
    for copy in weight_copies:
        copy.wait()


def prepare(basis, weights, pieces, blocks, bits):
    depth, rows = basis.shape
    wide = min(depth, COLUMNS)
    sems = pltpu.SemaphoreType.DMA((depth // wide,))
    return call(
        functools.partial(prepare_kernel, pieces, blocks, bits, wide),
        "split_basis",
        [basis, weights],
        [
            jax.ShapeDtypeStruct((2 * rows, depth), jnp.bfloat16),
            jax.ShapeDtypeStruct((depth, weights.shape[2]), jnp.bfloat16),
        ],
        [],
        [
            pltpu.VMEM((depth, rows), jnp.float32),
            pltpu.VMEM((rows, depth), jnp.float32),
            sems,
            sems,
        ],
        limit=10,
        cost=(2 * depth * rows, 8 * depth * rows, 0),
        far=2,
    )


def spans(width, wide):
    return [(at, min(wide, width - at)) for at in range(0, width, wide)]


def halves_added(product):
    half = product.shape[0] // 2
    return product[:half] + product[half:]


def early_kernel(pieces, width, own_ref, near_ref, w_ref, *refs):
    *other_refs, partial_ref, sems = refs
    depth = own_ref.shape[1]
    wide = min(depth, COLUMNS)
    copies = []
    for distance in range(1, pieces):
        copies += row_copies(
            w_ref, other_refs[distance - 1], sems.at[distance - 1], pieces, distance, wide
        )
    for copy in copies:
        copy.start()
    for at, wide in spans(width, COLUMNS):
        columns = slice(at, at + wide)
        part = jnp.dot(own_ref[...], near_ref[:, columns], preferred_element_type=jnp.float32)
        partial_ref[:, columns] = halves_added(part)
    for copy in copies:
        copy.wait()


def early(own, near, weights, pieces, width):
    rows2, depth = own.shape
    full = weights.shape[2]
    out = call(
        functools.partial(early_kernel, pieces, width),
        "early_products",
        [own, near, weights],
        [jax.ShapeDtypeStruct((depth, full), jnp.bfloat16)] * (pieces - 1)
        + [jax.ShapeDtypeStruct((rows2 // 2, width), jnp.float32)],
        [],
        [pltpu.SemaphoreType.DMA((pieces - 1, depth // min(depth, COLUMNS)))],
        limit=8,
        cost=(2 * rows2 * depth * width, 2 * pieces * depth * full, 0),
        far=1,
    )
    return [near, *out[:-1]], out[-1]


def product_kernel(pieces, start, width, early, step, leave, stay, *refs):
    left, right = refs[:pieces], refs[pieces : 2 * pieces]
    message_ref, kept_ref = refs[-2:]
    first = 1 if early else 0
    bounds = []
    for at, wide in spans(width, COLUMNS):
        columns = slice(start + at, start + at + wide)
        total = jnp.dot(
            jnp.concatenate([a_ref[...] for a_ref in left[first:]], axis=1),
            jnp.concatenate([w_ref[:, columns] for w_ref in right[first:]], axis=0),
            preferred_element_type=jnp.float32,
        )
        total = halves_added(total)
        if early:
            total = total + refs[2 * pieces][:, columns]
        for lane in range(0, wide, LANES):
            column = total[:, lane : lane + LANES]
            blocks = {p: column[p * step : (p + 1) * step] for p in leave + stay}
            tile = (at + lane) // LANES
            bounds.append(put_tile(message_ref, kept_ref, tile, blocks, step, leave, stay))
    put_bounds(message_ref, bounds, len(leave) * step)


def outputs(width, step, leave, stay):
    tiles = width // LANES
    sent = tiles * len(leave) * step + scale_rows(tiles)
    return [
        jax.ShapeDtypeStruct((sent, LANES), jnp.bfloat16),
        jax.ShapeDtypeStruct((tiles * len(stay) * step, LANES), jnp.float32),
    ]


def product(left, right, partial, start, width, step, leave, stay, after):
    rows2, depth = left[0].shape
    pieces = len(left)
    early = partial is not None
    count = pieces - 1 if early else pieces
    return call(
        functools.partial(product_kernel, pieces, start, width, early, step, leave, stay),
        "product",
        [*left, *right] + ([partial] if early else []),
        outputs(width, step, leave, stay),
        after,
        limit=8,
        cost=(
            2 * rows2 * depth * count * width,
            2 * depth * count * width + 4 * rows2 * width,
            rows2 * width // 4,
        ),
    )


def received(message_ref, kept_ref, tile, tiles, count):
    coded = message_ref[tile * count : (tile + 1) * count, :]
    group = tile // SCALE_ROWS * SCALE_ROWS
    at = tiles * count + group
    bounds = message_ref[at : at + SCALE_ROWS, :].astype(jnp.float32)
    bound = bounds[tile - group : tile - group + 1]
    return kept_ref[tile * count : (tile + 1) * count, :] + decode(coded, bound)


def middle_kernel(tiles, step, old, leave, stay, message_ref, kept_ref, out_ref, next_ref):
    bounds = []
    for tile in range(tiles):
        column = received(message_ref, kept_ref, tile, tiles, len(old) * step)
        blocks = {p: column[i * step : (i + 1) * step] for i, p in enumerate(old)}
        bounds.append(put_tile(out_ref, next_ref, tile, blocks, step, leave, stay))
    put_bounds(out_ref, bounds, len(leave) * step)


def middle(message, kept, width, step, old, leave, stay, after):
    size = width * len(old) * step
    return call(
        functools.partial(middle_kernel, width // LANES, step, old, leave, stay),
        "add_and_split",
        [message, kept],
        outputs(width, step, leave, stay),
        after,
        cost=(20 * size, 9 * size, 2 * size),
    )


def last_kernel(tiles, pieces, message_ref, kept_ref, *refs):
    outs = refs[:pieces]
    whole = refs[pieces]
    count = whole.shape[0]
    share = count // pieces
    for tile in range(tiles):
        whole[:, tile * LANES : (tile + 1) * LANES] = received(
            message_ref, kept_ref, tile, tiles, count
        )
    for distance in range(pieces):
        owner = jnp.bitwise_xor(position(pieces)[0], distance)
        rows = whole[pl.ds(pl.multiple_of(owner * share, share), share), :]
        outs[distance][...] = rows.astype(jnp.bfloat16)


def last(message, kept, width, step, pieces, after):
    size = width * step
    share = jax.ShapeDtypeStruct((step // pieces, width), jnp.bfloat16)
    return call(
        functools.partial(last_kernel, width // LANES, pieces),
        "add_last",
        [message, kept],
        [share] * pieces,
        after,
        [pltpu.VMEM((step, width), jnp.float32)],
        cost=(10 * size, 8 * size, size),
    )


def lay_kernel(pieces, width, *refs):
    out_ref = refs[-1]
    at = 0
    for first in range(0, len(refs) - 1, pieces):
        for distance in range(pieces):
            part = refs[first + distance]
            owner = jnp.bitwise_xor(position(pieces)[0], distance)
            columns = pl.ds(pl.multiple_of(owner * width + at, LANES), part.shape[1])
            out_ref[:, columns] = part[...]
        at += part.shape[1]


def lay(parts, pieces, width):
    flat = [part for chunk in parts for part in chunk]
    rows = flat[0].shape[0]
    return call(
        functools.partial(lay_kernel, pieces, width),
        "lay_out",
        [*flat],
        [jax.ShapeDtypeStruct((rows, pieces * width), jnp.bfloat16)],
        [],
        cost=(0, 4 * rows * pieces * width, 0),
    )[0]


def swapped(block, apart):
    count = lax.axis_size("row")
    return lax.ppermute(block, "row", [(i, i ^ apart) for i in range(count)])


def on_device(basis, weights):
    axis_len = lax.axis_size("row")
    depth, rows = basis.shape
    pieces = weights.shape[1] // depth
    blocks = axis_len // pieces
    bits = blocks.bit_length() - 1
    step = rows // blocks
    width = weights.shape[2]

    own, near = prepare(basis, weights, pieces, blocks, bits)
    left = [own] + [swapped(own, distance) for distance in range(1, pieces)]

    cuts = [0]
    for share, _ in CHUNKS:
        cuts.append(cuts[-1] + share)
    cuts = [cut * (width // LANES) // PARTS * LANES for cut in cuts]
    orders = [[bit for bit in order if bit < bits] for _, order in CHUNKS]
    stages = [split_places(order, bits) for order in orders]
    right, partial = early(own, near, weights, pieces, cuts[EARLY])

    state = {}
    after = [partial]
    finished = {}
    for index, number in ORDER:
        order = orders[index]
        start = cuts[index]
        chunk = cuts[index + 1] - start
        if number == 0:
            begun = partial if index < EARLY else None
            out = product(
                left, right, begun, start, chunk, step, *stages[index][0], after
            )
        elif number < bits:
            message, kept = state[index]
            old = stages[index][number - 1][1]
            out = middle(message, kept, chunk, step, old, *stages[index][number], after)
        else:
            message, kept = state[index]
            out = last(message, kept, chunk, step, pieces, after)
            finished[index] = [out[0]] + [swapped(out[d], d) for d in range(1, pieces)]
            after = [out[0]]
            continue
        state[index] = swapped(out[0], pieces << order[number]), out[1]
        after = [out[1]]
    return lay([finished[index] for index in sorted(finished)], pieces, width)


def solution(mesh):
    in_specs = (P(("groups", "row"), None), P(("groups", "row"), None, None))
    out_specs = P(("groups", "row"), None)
    return jax.shard_map(
        on_device, mesh=mesh, in_specs=in_specs, out_specs=out_specs, check_vma=False
    )
```

```python
import functools

import jax
import jax.numpy as jnp
from jax import lax
from jax.experimental import pallas as pl
from jax.experimental.pallas import tpu as pltpu
from jax.sharding import PartitionSpec as P

LANES = 128
SCALE_ROWS = 16
COLUMNS = 256
TILE = 512
HALF_SPAN = 125.0
SPAN = 250.0
TINY = 2.0**-110
MIB = 1 << 20

CHUNKS = [
    (4, (0, 2, 1)),
    (4, (1, 0, 2)),
    (4, (0, 2, 1)),
    (2, (1, 0, 2)),
    (2, (0, 1, 2)),
]
PARTS = 16
EARLY = 1
ORDER = [
    (0, 0), (1, 0), (2, 0), (0, 1), (3, 0), (4, 0), (1, 1), (2, 1),
    (0, 2), (3, 1), (4, 1), (1, 2), (2, 2), (0, 3), (3, 2), (4, 2),
    (1, 3), (2, 3), (3, 3), (4, 3),
]


def column_bound(values):
    top = jnp.maximum(jnp.max(jnp.abs(values), axis=0, keepdims=True), TINY)
    return (top * 1.008).astype(jnp.bfloat16).astype(jnp.float32)


def encode(values, bound):
    level = jnp.exp2(jnp.abs(values) * (SPAN / bound) - HALF_SPAN)
    return jnp.where(values < 0, -level, level).astype(jnp.bfloat16)


def decode(coded, bound):
    coded = coded.astype(jnp.float32)
    size = (jnp.log2(jnp.abs(coded)) + HALF_SPAN) * (bound * (1.0 / SPAN))
    return jnp.where(coded < 0, -size, size)


def reversed_bits(value, bits):
    out = 0
    for bit in range(bits):
        out |= (value >> bit & 1) << (bits - 1 - bit)
    return out


def split_places(order, bits):
    stay = list(range(1 << bits))
    stages = []
    for bit in order:
        leave = [p for p in stay if reversed_bits(p, bits) >> bit & 1]
        stay = [p for p in stay if not reversed_bits(p, bits) >> bit & 1]
        stages.append((leave, stay))
    return stages


def scale_rows(tiles):
    return -(-tiles // SCALE_ROWS) * SCALE_ROWS


def put_bounds(message_ref, bounds, count):
    tiles = len(bounds)
    spare = scale_rows(tiles) - tiles
    if spare:
        bounds = bounds + [jnp.zeros((spare, LANES), jnp.float32)]
    message_ref[tiles * count :, :] = jnp.concatenate(bounds, axis=0).astype(jnp.bfloat16)


def put_tile(message_ref, kept_ref, tile, blocks, step, leave, stay):
    sent = jnp.concatenate([blocks[p] for p in leave], axis=0)
    bound = column_bound(sent)
    count = len(leave) * step
    message_ref[tile * count : (tile + 1) * count, :] = encode(sent, bound)
    for slot, p in enumerate(stay):
        at = (tile * len(stay) + slot) * step
        kept_ref[at : at + step, :] = blocks[p]
    return bound


def position(pieces):
    me = lax.axis_index("row").astype(jnp.int32)
    return jnp.bitwise_and(me, pieces - 1), jnp.right_shift(me, pieces.bit_length() - 1)


def call(kernel, name, ins, outs, after, scratch=(), limit=4, cost=(0, 0, 0), far=0):
    count = len(ins)

    def run(*refs):
        kernel(*refs[:count], *refs[count + len(after) :])

    vmem = pl.BlockSpec(memory_space=pltpu.VMEM)
    near = count - far
    ins = ins[:near] + [pltpu.with_memory_space_constraint(x, pltpu.HBM) for x in ins[near:]]
    return pl.pallas_call(
        run,
        in_specs=[vmem] * (count - far)
        + [pl.BlockSpec(memory_space=pltpu.HBM)] * far
        + [pl.BlockSpec(memory_space=pl.ANY)] * len(after),
        out_specs=[vmem] * len(outs),
        out_shape=outs,
        scratch_shapes=scratch,
        compiler_params=pltpu.CompilerParams(vmem_limit_bytes=limit * MIB),
        cost_estimate=pl.CostEstimate(flops=1, bytes_accessed=1, transcendentals=0),
        name=name,
    )(*ins, *after)


def row_copies(w_ref, near_ref, sems, pieces, distance, wide):
    depth = near_ref.shape[0]
    owner = jnp.bitwise_xor(position(pieces)[0], distance)
    copies = []
    for index, at in enumerate(range(0, depth, wide)):
        source = pl.ds(pl.multiple_of(owner * depth + at, wide), wide)
        copies.append(
            pltpu.make_async_copy(
                w_ref.at[0, source, :], near_ref.at[pl.ds(at, wide), :], sems.at[index]
            )
        )
    return copies


def prepare_kernel(
    pieces, blocks, bits, wide, basis_ref, w_ref, out_ref, near_ref, held, turned, sems, w_sems
):
    depth, rows = basis_ref.shape
    step = rows // blocks
    mine = position(pieces)[1]
    copies = []
    for index, at in enumerate(range(0, depth, wide)):
        part = pl.ds(at, wide)
        copies.append(
            pltpu.make_async_copy(basis_ref.at[part, :], held.at[part, :], sems.at[index])
        )
    weight_copies = row_copies(w_ref, near_ref, w_sems, pieces, 0, wide)
    for copy in copies + weight_copies:
        copy.start()
    for index, at in enumerate(range(0, depth, wide)):
        copies[index].wait()
        turned[:, at : at + wide] = held[at : at + wide, :].T
        for place in range(blocks):
            source = jnp.bitwise_xor(mine, reversed_bits(place, bits))
            part = turned[pl.ds(pl.multiple_of(source * step, step), step), at : at + wide]
            high = part.astype(jnp.bfloat16)
            low = (part - high.astype(jnp.float32)).astype(jnp.bfloat16)
            out_ref[place * step : (place + 1) * step, at : at + wide] = high
            out_ref[rows + place * step : rows + (place + 1) * step, at : at + wide] = low
    for copy in weight_copies:
        copy.wait()


def prepare(basis, weights, pieces, blocks, bits):
    depth, rows = basis.shape
    wide = min(depth, COLUMNS)
    sems = pltpu.SemaphoreType.DMA((depth // wide,))
    return call(
        functools.partial(prepare_kernel, pieces, blocks, bits, wide),
        "split_basis",
        [basis, weights],
        [
            jax.ShapeDtypeStruct((2 * rows, depth), jnp.bfloat16),
            jax.ShapeDtypeStruct((depth, weights.shape[2]), jnp.bfloat16),
        ],
        [],
        [
            pltpu.VMEM((depth, rows), jnp.float32),
            pltpu.VMEM((rows, depth), jnp.float32),
            sems,
            sems,
        ],
        limit=10,
        cost=(2 * depth * rows, 8 * depth * rows, 0),
        far=2,
    )


def spans(width, wide):
    return [(at, min(wide, width - at)) for at in range(0, width, wide)]


def halves_added(product):
    half = product.shape[0] // 2
    return product[:half] + product[half:]


def early_kernel(pieces, width, own_ref, near_ref, w_ref, *refs):
    *other_refs, partial_ref, sems = refs
    depth = own_ref.shape[1]
    wide = min(depth, COLUMNS)
    copies = []
    for distance in range(1, pieces):
        copies += row_copies(
            w_ref, other_refs[distance - 1], sems.at[distance - 1], pieces, distance, wide
        )
    for copy in copies:
        copy.start()
    for at, wide in spans(width, TILE):
        columns = slice(at, at + wide)
        part = jnp.dot(own_ref[...], near_ref[:, columns], preferred_element_type=jnp.float32)
        partial_ref[:, columns] = halves_added(part)
    for copy in copies:
        copy.wait()


def early(own, near, weights, pieces, width):
    rows2, depth = own.shape
    full = weights.shape[2]
    out = call(
        functools.partial(early_kernel, pieces, width),
        "early_products",
        [own, near, weights],
        [jax.ShapeDtypeStruct((depth, full), jnp.bfloat16)] * (pieces - 1)
        + [jax.ShapeDtypeStruct((rows2 // 2, width), jnp.float32)],
        [],
        [pltpu.SemaphoreType.DMA((pieces - 1, depth // min(depth, COLUMNS)))],
        limit=12,
        cost=(2 * rows2 * depth * width, 2 * pieces * depth * full, 0),
        far=1,
    )
    return [near, *out[:-1]], out[-1]


def product_kernel(pieces, start, width, early, step, leave, stay, *refs):
    left, right = refs[:pieces], refs[pieces : 2 * pieces]
    message_ref, kept_ref = refs[-2:]
    first = 1 if early else 0
    bounds = []
    for at, wide in spans(width, TILE):
        columns = slice(start + at, start + at + wide)
        total = jnp.dot(
            jnp.concatenate([a_ref[...] for a_ref in left[first:]], axis=1),
            jnp.concatenate([w_ref[:, columns] for w_ref in right[first:]], axis=0),
            preferred_element_type=jnp.float32,
        )
        total = halves_added(total)
        if early:
            total = total + refs[2 * pieces][:, columns]
        for lane in range(0, wide, LANES):
            column = total[:, lane : lane + LANES]
            blocks = {p: column[p * step : (p + 1) * step] for p in leave + stay}
            tile = (at + lane) // LANES
            bounds.append(put_tile(message_ref, kept_ref, tile, blocks, step, leave, stay))
    put_bounds(message_ref, bounds, len(leave) * step)


def outputs(width, step, leave, stay):
    tiles = width // LANES
    sent = tiles * len(leave) * step + scale_rows(tiles)
    return [
        jax.ShapeDtypeStruct((sent, LANES), jnp.bfloat16),
        jax.ShapeDtypeStruct((tiles * len(stay) * step, LANES), jnp.float32),
    ]


def product(left, right, partial, start, width, step, leave, stay, after):
    rows2, depth = left[0].shape
    pieces = len(left)
    early = partial is not None
    count = pieces - 1 if early else pieces
    return call(
        functools.partial(product_kernel, pieces, start, width, early, step, leave, stay),
        "product",
        [*left, *right] + ([partial] if early else []),
        outputs(width, step, leave, stay),
        after,
        limit=12,
        cost=(
            2 * rows2 * depth * count * width,
            2 * depth * count * width + 4 * rows2 * width,
            rows2 * width // 4,
        ),
    )


def received(message_ref, kept_ref, tile, tiles, count):
    coded = message_ref[tile * count : (tile + 1) * count, :]
    group = tile // SCALE_ROWS * SCALE_ROWS
    at = tiles * count + group
    bounds = message_ref[at : at + SCALE_ROWS, :].astype(jnp.float32)
    bound = bounds[tile - group : tile - group + 1]
    return kept_ref[tile * count : (tile + 1) * count, :] + decode(coded, bound)


def middle_kernel(tiles, step, old, leave, stay, message_ref, kept_ref, out_ref, next_ref):
    bounds = []
    for tile in range(tiles):
        column = received(message_ref, kept_ref, tile, tiles, len(old) * step)
        blocks = {p: column[i * step : (i + 1) * step] for i, p in enumerate(old)}
        bounds.append(put_tile(out_ref, next_ref, tile, blocks, step, leave, stay))
    put_bounds(out_ref, bounds, len(leave) * step)


def middle(message, kept, width, step, old, leave, stay, after):
    size = width * len(old) * step
    return call(
        functools.partial(middle_kernel, width // LANES, step, old, leave, stay),
        "add_and_split",
        [message, kept],
        outputs(width, step, leave, stay),
        after,
        cost=(20 * size, 9 * size, 2 * size),
    )


def last_kernel(tiles, pieces, message_ref, kept_ref, *refs):
    outs = refs[:pieces]
    whole = refs[pieces]
    count = whole.shape[0]
    share = count // pieces
    for tile in range(tiles):
        whole[:, tile * LANES : (tile + 1) * LANES] = received(
            message_ref, kept_ref, tile, tiles, count
        )
    for distance in range(pieces):
        owner = jnp.bitwise_xor(position(pieces)[0], distance)
        rows = whole[pl.ds(pl.multiple_of(owner * share, share), share), :]
        outs[distance][...] = rows.astype(jnp.bfloat16)


def last(message, kept, width, step, pieces, after):
    size = width * step
    share = jax.ShapeDtypeStruct((step // pieces, width), jnp.bfloat16)
    return call(
        functools.partial(last_kernel, width // LANES, pieces),
        "add_last",
        [message, kept],
        [share] * pieces,
        after,
        [pltpu.VMEM((step, width), jnp.float32)],
        cost=(10 * size, 8 * size, size),
    )


def lay_kernel(pieces, width, *refs):
    out_ref = refs[-1]
    at = 0
    for first in range(0, len(refs) - 1, pieces):
        for distance in range(pieces):
            part = refs[first + distance]
            owner = jnp.bitwise_xor(position(pieces)[0], distance)
            columns = pl.ds(pl.multiple_of(owner * width + at, LANES), part.shape[1])
            out_ref[:, columns] = part[...]
        at += part.shape[1]


def lay(parts, pieces, width):
    flat = [part for chunk in parts for part in chunk]
    rows = flat[0].shape[0]
    return call(
        functools.partial(lay_kernel, pieces, width),
        "lay_out",
        [*flat],
        [jax.ShapeDtypeStruct((rows, pieces * width), jnp.bfloat16)],
        [],
        cost=(0, 4 * rows * pieces * width, 0),
    )[0]


def swapped(block, apart):
    count = lax.axis_size("row")
    return lax.ppermute(block, "row", [(i, i ^ apart) for i in range(count)])


def on_device(basis, weights):
    axis_len = lax.axis_size("row")
    depth, rows = basis.shape
    pieces = weights.shape[1] // depth
    blocks = axis_len // pieces
    bits = blocks.bit_length() - 1
    step = rows // blocks
    width = weights.shape[2]

    own, near = prepare(basis, weights, pieces, blocks, bits)
    left = [own] + [swapped(own, distance) for distance in range(1, pieces)]

    cuts = [0]
    for share, _ in CHUNKS:
        cuts.append(cuts[-1] + share)
    cuts = [cut * (width // LANES) // PARTS * LANES for cut in cuts]
    orders = [[bit for bit in order if bit < bits] for _, order in CHUNKS]
    stages = [split_places(order, bits) for order in orders]
    right, partial = early(own, near, weights, pieces, cuts[EARLY])

    state = {}
    after = [partial]
    finished = {}
    for index, number in ORDER:
        order = orders[index]
        start = cuts[index]
        chunk = cuts[index + 1] - start
        if number == 0:
            begun = partial if index < EARLY else None
            out = product(
                left, right, begun, start, chunk, step, *stages[index][0], after
            )
        elif number < bits:
            message, kept = state[index]
            old = stages[index][number - 1][1]
            out = middle(message, kept, chunk, step, old, *stages[index][number], after)
        else:
            message, kept = state[index]
            out = last(message, kept, chunk, step, pieces, after)
            finished[index] = [out[0]] + [swapped(out[d], d) for d in range(1, pieces)]
            after = [out[0]]
            continue
        state[index] = swapped(out[0], pieces << order[number]), out[1]
        after = [out[1]]
    return lay([finished[index] for index in sorted(finished)], pieces, width)


def solution(mesh):
    in_specs = (P(("groups", "row"), None), P(("groups", "row"), None, None))
    out_specs = P(("groups", "row"), None)
    return jax.shard_map(
        on_device, mesh=mesh, in_specs=in_specs, out_specs=out_specs, check_vma=False
    )
```

```python
import functools

import jax
import jax.numpy as jnp
from jax import lax
from jax.experimental import pallas as pl
from jax.experimental.pallas import tpu as pltpu
from jax.sharding import PartitionSpec as P

LANES = 128
SCALE_ROWS = 16
COLUMNS = 256
TILE = 512
HALF_SPAN = 125.0
SPAN = 250.0
TINY = 2.0**-110
MIB = 1 << 20

CHUNKS = [
    (4, (0, 2, 1)),
    (4, (1, 0, 2)),
    (4, (0, 2, 1)),
    (2, (1, 0, 2)),
    (2, (0, 1, 2)),
]
PARTS = 16
EARLY = 2
ORDER = [
    (0, 0), (1, 0), (2, 0), (0, 1), (3, 0), (4, 0), (1, 1), (2, 1),
    (0, 2), (3, 1), (4, 1), (1, 2), (2, 2), (0, 3), (3, 2), (4, 2),
    (1, 3), (2, 3), (3, 3), (4, 3),
]


def column_bound(values):
    top = jnp.maximum(jnp.max(jnp.abs(values), axis=0, keepdims=True), TINY)
    return (top * 1.008).astype(jnp.bfloat16).astype(jnp.float32)


def encode(values, bound):
    level = jnp.exp2(jnp.abs(values) * (SPAN / bound) - HALF_SPAN)
    return jnp.where(values < 0, -level, level).astype(jnp.bfloat16)


def decode(coded, bound):
    coded = coded.astype(jnp.float32)
    size = (jnp.log2(jnp.abs(coded)) + HALF_SPAN) * (bound * (1.0 / SPAN))
    return jnp.where(coded < 0, -size, size)


def reversed_bits(value, bits):
    out = 0
    for bit in range(bits):
        out |= (value >> bit & 1) << (bits - 1 - bit)
    return out


def split_places(order, bits):
    stay = list(range(1 << bits))
    stages = []
    for bit in order:
        leave = [p for p in stay if reversed_bits(p, bits) >> bit & 1]
        stay = [p for p in stay if not reversed_bits(p, bits) >> bit & 1]
        stages.append((leave, stay))
    return stages


def scale_rows(tiles):
    return -(-tiles // SCALE_ROWS) * SCALE_ROWS


def put_bounds(message_ref, bounds, count):
    tiles = len(bounds)
    spare = scale_rows(tiles) - tiles
    if spare:
        bounds = bounds + [jnp.zeros((spare, LANES), jnp.float32)]
    message_ref[tiles * count :, :] = jnp.concatenate(bounds, axis=0).astype(jnp.bfloat16)


def put_tile(message_ref, kept_ref, tile, blocks, step, leave, stay):
    sent = jnp.concatenate([blocks[p] for p in leave], axis=0)
    bound = column_bound(sent)
    count = len(leave) * step
    message_ref[tile * count : (tile + 1) * count, :] = encode(sent, bound)
    for slot, p in enumerate(stay):
        at = (tile * len(stay) + slot) * step
        kept_ref[at : at + step, :] = blocks[p]
    return bound


def position(pieces):
    me = lax.axis_index("row").astype(jnp.int32)
    return jnp.bitwise_and(me, pieces - 1), jnp.right_shift(me, pieces.bit_length() - 1)


def call(kernel, name, ins, outs, after, scratch=(), limit=4, cost=(0, 0, 0), far=0):
    count = len(ins)

    def run(*refs):
        kernel(*refs[:count], *refs[count + len(after) :])

    vmem = pl.BlockSpec(memory_space=pltpu.VMEM)
    near = count - far
    ins = ins[:near] + [pltpu.with_memory_space_constraint(x, pltpu.HBM) for x in ins[near:]]
    return pl.pallas_call(
        run,
        in_specs=[vmem] * (count - far)
        + [pl.BlockSpec(memory_space=pltpu.HBM)] * far
        + [pl.BlockSpec(memory_space=pl.ANY)] * len(after),
        out_specs=[vmem] * len(outs),
        out_shape=outs,
        scratch_shapes=scratch,
        compiler_params=pltpu.CompilerParams(vmem_limit_bytes=limit * MIB),
        cost_estimate=pl.CostEstimate(flops=1, bytes_accessed=1, transcendentals=0),
        name=name,
    )(*ins, *after)


def row_copies(w_ref, near_ref, sems, pieces, distance, wide):
    depth = near_ref.shape[0]
    owner = jnp.bitwise_xor(position(pieces)[0], distance)
    copies = []
    for index, at in enumerate(range(0, depth, wide)):
        source = pl.ds(pl.multiple_of(owner * depth + at, wide), wide)
        copies.append(
            pltpu.make_async_copy(
                w_ref.at[0, source, :], near_ref.at[pl.ds(at, wide), :], sems.at[index]
            )
        )
    return copies


def prepare_kernel(
    pieces, blocks, bits, wide, basis_ref, w_ref, out_ref, near_ref, held, turned, sems, w_sems
):
    depth, rows = basis_ref.shape
    step = rows // blocks
    mine = position(pieces)[1]
    copies = []
    for index, at in enumerate(range(0, depth, wide)):
        part = pl.ds(at, wide)
        copies.append(
            pltpu.make_async_copy(basis_ref.at[part, :], held.at[part, :], sems.at[index])
        )
    weight_copies = row_copies(w_ref, near_ref, w_sems, pieces, 0, wide)
    for copy in copies + weight_copies:
        copy.start()
    for index, at in enumerate(range(0, depth, wide)):
        copies[index].wait()
        turned[:, at : at + wide] = held[at : at + wide, :].T
        for place in range(blocks):
            source = jnp.bitwise_xor(mine, reversed_bits(place, bits))
            part = turned[pl.ds(pl.multiple_of(source * step, step), step), at : at + wide]
            high = part.astype(jnp.bfloat16)
            low = (part - high.astype(jnp.float32)).astype(jnp.bfloat16)
            out_ref[place * step : (place + 1) * step, at : at + wide] = high
            out_ref[rows + place * step : rows + (place + 1) * step, at : at + wide] = low
    for copy in weight_copies:
        copy.wait()


def prepare(basis, weights, pieces, blocks, bits):
    depth, rows = basis.shape
    wide = min(depth, COLUMNS)
    sems = pltpu.SemaphoreType.DMA((depth // wide,))
    return call(
        functools.partial(prepare_kernel, pieces, blocks, bits, wide),
        "split_basis",
        [basis, weights],
        [
            jax.ShapeDtypeStruct((2 * rows, depth), jnp.bfloat16),
            jax.ShapeDtypeStruct((depth, weights.shape[2]), jnp.bfloat16),
        ],
        [],
        [
            pltpu.VMEM((depth, rows), jnp.float32),
            pltpu.VMEM((rows, depth), jnp.float32),
            sems,
            sems,
        ],
        limit=10,
        cost=(2 * depth * rows, 8 * depth * rows, 0),
        far=2,
    )


def spans(width, wide):
    return [(at, min(wide, width - at)) for at in range(0, width, wide)]


def halves_added(product):
    half = product.shape[0] // 2
    return product[:half] + product[half:]


def early_kernel(pieces, width, own_ref, near_ref, w_ref, *refs):
    *other_refs, partial_ref, sems = refs
    depth = own_ref.shape[1]
    wide = min(depth, COLUMNS)
    copies = []
    for distance in range(1, pieces):
        copies += row_copies(
            w_ref, other_refs[distance - 1], sems.at[distance - 1], pieces, distance, wide
        )
    for copy in copies:
        copy.start()

    def multiply(columns):
        part = jnp.dot(own_ref[...], near_ref[:, columns], preferred_element_type=jnp.float32)
        partial_ref[:, columns] = halves_added(part)

    tiles = width // COLUMNS

    @pl.loop(0, tiles)
    def _(tile):
        multiply(pl.ds(pl.multiple_of(tile * COLUMNS, COLUMNS), COLUMNS))

    if tiles * COLUMNS < width:
        multiply(slice(tiles * COLUMNS, width))
    for copy in copies:
        copy.wait()


def early(own, near, weights, pieces, width):
    rows2, depth = own.shape
    full = weights.shape[2]
    out = call(
        functools.partial(early_kernel, pieces, width),
        "early_products",
        [own, near, weights],
        [jax.ShapeDtypeStruct((depth, full), jnp.bfloat16)] * (pieces - 1)
        + [jax.ShapeDtypeStruct((rows2 // 2, width), jnp.float32)],
        [],
        [pltpu.SemaphoreType.DMA((pieces - 1, depth // min(depth, COLUMNS)))],
        limit=12,
        cost=(2 * rows2 * depth * width, 2 * pieces * depth * full, 0),
        far=1,
    )
    return [near, *out[:-1]], out[-1]


def product_kernel(pieces, start, width, early, step, leave, stay, *refs):
    left, right = refs[:pieces], refs[pieces : 2 * pieces]
    message_ref, kept_ref = refs[-2:]
    first = 1 if early else 0
    bounds = []
    for at, wide in spans(width, TILE):
        columns = slice(start + at, start + at + wide)
        total = jnp.dot(
            jnp.concatenate([a_ref[...] for a_ref in left[first:]], axis=1),
            jnp.concatenate([w_ref[:, columns] for w_ref in right[first:]], axis=0),
            preferred_element_type=jnp.float32,
        )
        total = halves_added(total)
        if early:
            total = total + refs[2 * pieces][:, columns]
        for lane in range(0, wide, LANES):
            column = total[:, lane : lane + LANES]
            blocks = {p: column[p * step : (p + 1) * step] for p in leave + stay}
            tile = (at + lane) // LANES
            bounds.append(put_tile(message_ref, kept_ref, tile, blocks, step, leave, stay))
    put_bounds(message_ref, bounds, len(leave) * step)


def outputs(width, step, leave, stay):
    tiles = width // LANES
    sent = tiles * len(leave) * step + scale_rows(tiles)
    return [
        jax.ShapeDtypeStruct((sent, LANES), jnp.bfloat16),
        jax.ShapeDtypeStruct((tiles * len(stay) * step, LANES), jnp.float32),
    ]


def product(left, right, partial, start, width, step, leave, stay, after):
    rows2, depth = left[0].shape
    pieces = len(left)
    early = partial is not None
    count = pieces - 1 if early else pieces
    return call(
        functools.partial(product_kernel, pieces, start, width, early, step, leave, stay),
        "product",
        [*left, *right] + ([partial] if early else []),
        outputs(width, step, leave, stay),
        after,
        limit=12,
        cost=(
            2 * rows2 * depth * count * width,
            2 * depth * count * width + 4 * rows2 * width,
            rows2 * width // 4,
        ),
    )


def received(message_ref, kept_ref, tile, tiles, count):
    coded = message_ref[tile * count : (tile + 1) * count, :]
    group = tile // SCALE_ROWS * SCALE_ROWS
    at = tiles * count + group
    bounds = message_ref[at : at + SCALE_ROWS, :].astype(jnp.float32)
    bound = bounds[tile - group : tile - group + 1]
    return kept_ref[tile * count : (tile + 1) * count, :] + decode(coded, bound)


def middle_kernel(tiles, step, old, leave, stay, message_ref, kept_ref, out_ref, next_ref):
    bounds = []
    for tile in range(tiles):
        column = received(message_ref, kept_ref, tile, tiles, len(old) * step)
        blocks = {p: column[i * step : (i + 1) * step] for i, p in enumerate(old)}
        bounds.append(put_tile(out_ref, next_ref, tile, blocks, step, leave, stay))
    put_bounds(out_ref, bounds, len(leave) * step)


def middle(message, kept, width, step, old, leave, stay, after):
    size = width * len(old) * step
    return call(
        functools.partial(middle_kernel, width // LANES, step, old, leave, stay),
        "add_and_split",
        [message, kept],
        outputs(width, step, leave, stay),
        after,
        cost=(20 * size, 9 * size, 2 * size),
    )


def last_kernel(tiles, pieces, message_ref, kept_ref, *refs):
    outs = refs[:pieces]
    whole = refs[pieces]
    count = whole.shape[0]
    share = count // pieces
    for tile in range(tiles):
        whole[:, tile * LANES : (tile + 1) * LANES] = received(
            message_ref, kept_ref, tile, tiles, count
        )
    for distance in range(pieces):
        owner = jnp.bitwise_xor(position(pieces)[0], distance)
        rows = whole[pl.ds(pl.multiple_of(owner * share, share), share), :]
        outs[distance][...] = rows.astype(jnp.bfloat16)


def last(message, kept, width, step, pieces, after):
    size = width * step
    share = jax.ShapeDtypeStruct((step // pieces, width), jnp.bfloat16)
    return call(
        functools.partial(last_kernel, width // LANES, pieces),
        "add_last",
        [message, kept],
        [share] * pieces,
        after,
        [pltpu.VMEM((step, width), jnp.float32)],
        cost=(10 * size, 8 * size, size),
    )


def lay_kernel(pieces, width, *refs):
    out_ref = refs[-1]
    at = 0
    for first in range(0, len(refs) - 1, pieces):
        for distance in range(pieces):
            part = refs[first + distance]
            owner = jnp.bitwise_xor(position(pieces)[0], distance)
            columns = pl.ds(pl.multiple_of(owner * width + at, LANES), part.shape[1])
            out_ref[:, columns] = part[...]
        at += part.shape[1]


def lay(parts, pieces, width):
    flat = [part for chunk in parts for part in chunk]
    rows = flat[0].shape[0]
    return call(
        functools.partial(lay_kernel, pieces, width),
        "lay_out",
        [*flat],
        [jax.ShapeDtypeStruct((rows, pieces * width), jnp.bfloat16)],
        [],
        cost=(0, 4 * rows * pieces * width, 0),
    )[0]


def swapped(block, apart):
    count = lax.axis_size("row")
    return lax.ppermute(block, "row", [(i, i ^ apart) for i in range(count)])


def on_device(basis, weights):
    axis_len = lax.axis_size("row")
    depth, rows = basis.shape
    pieces = weights.shape[1] // depth
    blocks = axis_len // pieces
    bits = blocks.bit_length() - 1
    step = rows // blocks
    width = weights.shape[2]

    own, near = prepare(basis, weights, pieces, blocks, bits)
    left = [own] + [swapped(own, distance) for distance in range(1, pieces)]

    cuts = [0]
    for share, _ in CHUNKS:
        cuts.append(cuts[-1] + share)
    cuts = [cut * (width // LANES) // PARTS * LANES for cut in cuts]
    orders = [[bit for bit in order if bit < bits] for _, order in CHUNKS]
    stages = [split_places(order, bits) for order in orders]
    right, partial = early(own, near, weights, pieces, cuts[EARLY])

    state = {}
    after = [partial]
    finished = {}
    for index, number in ORDER:
        order = orders[index]
        start = cuts[index]
        chunk = cuts[index + 1] - start
        if number == 0:
            begun = partial if index < EARLY else None
            out = product(
                left, right, begun, start, chunk, step, *stages[index][0], after
            )
        elif number < bits:
            message, kept = state[index]
            old = stages[index][number - 1][1]
            out = middle(message, kept, chunk, step, old, *stages[index][number], after)
        else:
            message, kept = state[index]
            out = last(message, kept, chunk, step, pieces, after)
            finished[index] = [out[0]] + [swapped(out[d], d) for d in range(1, pieces)]
            after = [out[0]]
            continue
        state[index] = swapped(out[0], pieces << order[number]), out[1]
        after = [out[1]]
    return lay([finished[index] for index in sorted(finished)], pieces, width)


def solution(mesh):
    in_specs = (P(("groups", "row"), None), P(("groups", "row"), None, None))
    out_specs = P(("groups", "row"), None)
    return jax.shard_map(
        on_device, mesh=mesh, in_specs=in_specs, out_specs=out_specs, check_vma=False
    )
```

```python
import functools

import jax
import jax.numpy as jnp
from jax import lax
from jax.experimental import pallas as pl
from jax.experimental.pallas import tpu as pltpu
from jax.sharding import PartitionSpec as P

LANES = 128
SCALE_ROWS = 16
COLUMNS = 256
TILE = 512
HALF_SPAN = 125.0
SPAN = 250.0
TINY = 2.0**-110
MIB = 1 << 20

CHUNKS = [
    (4, (0, 2, 1)),
    (4, (1, 0, 2)),
    (4, (0, 2, 1)),
    (2, (1, 0, 2)),
    (2, (0, 1, 2)),
]
PARTS = 16
EARLY = 2
ORDER = [
    (0, 0), (1, 0), (2, 0), (0, 1), (3, 0), (4, 0), (1, 1), (2, 1),
    (0, 2), (3, 1), (4, 1), (1, 2), (2, 2), (0, 3), (3, 2), (4, 2),
    (1, 3), (2, 3), (3, 3), (4, 3),
]


def column_bound(values):
    top = jnp.maximum(jnp.max(jnp.abs(values), axis=0, keepdims=True), TINY)
    return (top * 1.008).astype(jnp.bfloat16).astype(jnp.float32)


def encode(values, bound):
    level = jnp.exp2(jnp.abs(values) * (SPAN / bound) - HALF_SPAN)
    return jnp.where(values < 0, -level, level).astype(jnp.bfloat16)


def decode(coded, bound):
    coded = coded.astype(jnp.float32)
    size = (jnp.log2(jnp.abs(coded)) + HALF_SPAN) * (bound * (1.0 / SPAN))
    return jnp.where(coded < 0, -size, size)


def reversed_bits(value, bits):
    out = 0
    for bit in range(bits):
        out |= (value >> bit & 1) << (bits - 1 - bit)
    return out


def split_places(order, bits):
    stay = list(range(1 << bits))
    stages = []
    for bit in order:
        leave = [p for p in stay if reversed_bits(p, bits) >> bit & 1]
        stay = [p for p in stay if not reversed_bits(p, bits) >> bit & 1]
        stages.append((leave, stay))
    return stages


def scale_rows(tiles):
    return -(-tiles // SCALE_ROWS) * SCALE_ROWS


def put_bounds(message_ref, bounds, count):
    tiles = len(bounds)
    spare = scale_rows(tiles) - tiles
    if spare:
        bounds = bounds + [jnp.zeros((spare, LANES), jnp.float32)]
    message_ref[tiles * count :, :] = jnp.concatenate(bounds, axis=0).astype(jnp.bfloat16)


def put_tile(message_ref, kept_ref, tile, blocks, step, leave, stay):
    sent = jnp.concatenate([blocks[p] for p in leave], axis=0)
    bound = column_bound(sent)
    count = len(leave) * step
    message_ref[tile * count : (tile + 1) * count, :] = encode(sent, bound)
    for slot, p in enumerate(stay):
        at = (tile * len(stay) + slot) * step
        kept_ref[at : at + step, :] = blocks[p]
    return bound


def position(pieces):
    me = lax.axis_index("row").astype(jnp.int32)
    return jnp.bitwise_and(me, pieces - 1), jnp.right_shift(me, pieces.bit_length() - 1)


def call(kernel, name, ins, outs, after, scratch=(), limit=4, cost=(0, 0, 0), far=0):
    count = len(ins)

    def run(*refs):
        kernel(*refs[:count], *refs[count + len(after) :])

    vmem = pl.BlockSpec(memory_space=pltpu.VMEM)
    near = count - far
    ins = ins[:near] + [pltpu.with_memory_space_constraint(x, pltpu.HBM) for x in ins[near:]]
    return pl.pallas_call(
        run,
        in_specs=[vmem] * (count - far)
        + [pl.BlockSpec(memory_space=pltpu.HBM)] * far
        + [pl.BlockSpec(memory_space=pl.ANY)] * len(after),
        out_specs=[vmem] * len(outs),
        out_shape=outs,
        scratch_shapes=scratch,
        compiler_params=pltpu.CompilerParams(vmem_limit_bytes=limit * MIB),
        cost_estimate=pl.CostEstimate(flops=1, bytes_accessed=1, transcendentals=0),
        name=name,
    )(*ins, *after)


def row_copies(w_ref, near_ref, sems, pieces, distance, wide, first=0):
    depth, width = near_ref.shape
    owner = jnp.bitwise_xor(position(pieces)[0], distance)
    copies = []
    for index, at in enumerate(range(0, depth, wide)):
        source = pl.ds(pl.multiple_of(owner * depth + at, wide), wide)
        copies.append(
            pltpu.make_async_copy(
                w_ref.at[0, source, pl.ds(first, width)],
                near_ref.at[pl.ds(at, wide), :],
                sems.at[index],
            )
        )
    return copies


def prepare_kernel(
    pieces, blocks, bits, wide, basis_ref, w_ref, out_ref, near_ref, held, turned, sems, w_sems
):
    depth, rows = basis_ref.shape
    step = rows // blocks
    mine = position(pieces)[1]
    copies = []
    for index, at in enumerate(range(0, depth, wide)):
        part = pl.ds(at, wide)
        copies.append(
            pltpu.make_async_copy(basis_ref.at[part, :], held.at[part, :], sems.at[index])
        )
    weight_copies = row_copies(w_ref, near_ref, w_sems, pieces, 0, wide)
    for copy in copies + weight_copies:
        copy.start()
    for index, at in enumerate(range(0, depth, wide)):
        copies[index].wait()
        turned[:, at : at + wide] = held[at : at + wide, :].T
        for place in range(blocks):
            source = jnp.bitwise_xor(mine, reversed_bits(place, bits))
            part = turned[pl.ds(pl.multiple_of(source * step, step), step), at : at + wide]
            high = part.astype(jnp.bfloat16)
            low = (part - high.astype(jnp.float32)).astype(jnp.bfloat16)
            out_ref[place * step : (place + 1) * step, at : at + wide] = high
            out_ref[rows + place * step : rows + (place + 1) * step, at : at + wide] = low
    for copy in weight_copies:
        copy.wait()


def prepare(basis, weights, pieces, blocks, bits, width):
    depth, rows = basis.shape
    wide = min(depth, COLUMNS)
    sems = pltpu.SemaphoreType.DMA((depth // wide,))
    return call(
        functools.partial(prepare_kernel, pieces, blocks, bits, wide),
        "split_basis",
        [basis, weights],
        [
            jax.ShapeDtypeStruct((2 * rows, depth), jnp.bfloat16),
            jax.ShapeDtypeStruct((depth, width), jnp.bfloat16),
        ],
        [],
        [
            pltpu.VMEM((depth, rows), jnp.float32),
            pltpu.VMEM((rows, depth), jnp.float32),
            sems,
            sems,
        ],
        limit=10,
        cost=(2 * depth * rows, 8 * depth * rows, 0),
        far=2,
    )


def spans(width, wide):
    return [(at, min(wide, width - at)) for at in range(0, width, wide)]


def halves_added(product):
    half = product.shape[0] // 2
    return product[:half] + product[half:]


def early_kernel(pieces, width, own_ref, near_ref, w_ref, *refs):
    *later_refs, partial_ref, sems = refs
    depth = own_ref.shape[1]
    wide = min(depth, COLUMNS)
    copies = []
    for distance in [*range(1, pieces), 0]:
        first = 0 if distance else width
        copies += row_copies(
            w_ref, later_refs[distance], sems.at[distance], pieces, distance, wide, first
        )
    for copy in copies:
        copy.start()

    def multiply(columns):
        part = jnp.dot(own_ref[...], near_ref[:, columns], preferred_element_type=jnp.float32)
        partial_ref[:, columns] = halves_added(part)

    tiles = width // COLUMNS

    @pl.loop(0, tiles)
    def _(tile):
        multiply(pl.ds(pl.multiple_of(tile * COLUMNS, COLUMNS), COLUMNS))

    if tiles * COLUMNS < width:
        multiply(slice(tiles * COLUMNS, width))
    for copy in copies:
        copy.wait()


def early(own, near, weights, pieces, width):
    rows2, depth = own.shape
    full = weights.shape[2]
    out = call(
        functools.partial(early_kernel, pieces, width),
        "early_products",
        [own, near, weights],
        [jax.ShapeDtypeStruct((depth, full - width), jnp.bfloat16)]
        + [jax.ShapeDtypeStruct((depth, full), jnp.bfloat16)] * (pieces - 1)
        + [jax.ShapeDtypeStruct((rows2 // 2, width), jnp.float32)],
        [],
        [pltpu.SemaphoreType.DMA((pieces, depth // min(depth, COLUMNS)))],
        limit=12,
        cost=(2 * rows2 * depth * width, 2 * pieces * depth * full, 0),
        far=1,
    )
    return out[:-1], out[-1]


def product_kernel(pieces, start, width, skip, early, step, leave, stay, *refs):
    left, right = refs[:pieces], refs[pieces : 2 * pieces]
    message_ref, kept_ref = refs[-2:]
    first = 1 if early else 0
    bounds = []
    for at, wide in spans(width, TILE):
        columns = slice(start + at, start + at + wide)
        own_columns = slice(columns.start - skip, columns.stop - skip)
        taken = [w_ref[:, columns] for w_ref in right[1:]]
        if not early:
            taken = [right[0][:, own_columns]] + taken
        total = jnp.dot(
            jnp.concatenate([a_ref[...] for a_ref in left[first:]], axis=1),
            jnp.concatenate(taken, axis=0),
            preferred_element_type=jnp.float32,
        )
        total = halves_added(total)
        if early:
            total = total + refs[2 * pieces][:, columns]
        for lane in range(0, wide, LANES):
            column = total[:, lane : lane + LANES]
            blocks = {p: column[p * step : (p + 1) * step] for p in leave + stay}
            tile = (at + lane) // LANES
            bounds.append(put_tile(message_ref, kept_ref, tile, blocks, step, leave, stay))
    put_bounds(message_ref, bounds, len(leave) * step)


def outputs(width, step, leave, stay):
    tiles = width // LANES
    sent = tiles * len(leave) * step + scale_rows(tiles)
    return [
        jax.ShapeDtypeStruct((sent, LANES), jnp.bfloat16),
        jax.ShapeDtypeStruct((tiles * len(stay) * step, LANES), jnp.float32),
    ]


def product(left, right, partial, start, width, step, leave, stay, after):
    rows2, depth = left[0].shape
    pieces = len(left)
    early = partial is not None
    skip = right[1].shape[1] - right[0].shape[1]
    count = pieces - 1 if early else pieces
    return call(
        functools.partial(product_kernel, pieces, start, width, skip, early, step, leave, stay),
        "product",
        [*left, *right] + ([partial] if early else []),
        outputs(width, step, leave, stay),
        after,
        limit=12,
        cost=(
            2 * rows2 * depth * count * width,
            2 * depth * count * width + 4 * rows2 * width,
            rows2 * width // 4,
        ),
    )


def received(message_ref, kept_ref, tile, tiles, count):
    coded = message_ref[tile * count : (tile + 1) * count, :]
    group = tile // SCALE_ROWS * SCALE_ROWS
    at = tiles * count + group
    bounds = message_ref[at : at + SCALE_ROWS, :].astype(jnp.float32)
    bound = bounds[tile - group : tile - group + 1]
    return kept_ref[tile * count : (tile + 1) * count, :] + decode(coded, bound)


def middle_kernel(tiles, step, old, leave, stay, message_ref, kept_ref, out_ref, next_ref):
    bounds = []
    for tile in range(tiles):
        column = received(message_ref, kept_ref, tile, tiles, len(old) * step)
        blocks = {p: column[i * step : (i + 1) * step] for i, p in enumerate(old)}
        bounds.append(put_tile(out_ref, next_ref, tile, blocks, step, leave, stay))
    put_bounds(out_ref, bounds, len(leave) * step)


def middle(message, kept, width, step, old, leave, stay, after):
    size = width * len(old) * step
    return call(
        functools.partial(middle_kernel, width // LANES, step, old, leave, stay),
        "add_and_split",
        [message, kept],
        outputs(width, step, leave, stay),
        after,
        cost=(20 * size, 9 * size, 2 * size),
    )


def last_kernel(tiles, pieces, message_ref, kept_ref, *refs):
    outs = refs[:pieces]
    whole = refs[pieces]
    count = whole.shape[0]
    share = count // pieces
    for tile in range(tiles):
        whole[:, tile * LANES : (tile + 1) * LANES] = received(
            message_ref, kept_ref, tile, tiles, count
        )
    for distance in range(pieces):
        owner = jnp.bitwise_xor(position(pieces)[0], distance)
        rows = whole[pl.ds(pl.multiple_of(owner * share, share), share), :]
        outs[distance][...] = rows.astype(jnp.bfloat16)


def last(message, kept, width, step, pieces, after):
    size = width * step
    share = jax.ShapeDtypeStruct((step // pieces, width), jnp.bfloat16)
    return call(
        functools.partial(last_kernel, width // LANES, pieces),
        "add_last",
        [message, kept],
        [share] * pieces,
        after,
        [pltpu.VMEM((step, width), jnp.float32)],
        cost=(10 * size, 8 * size, size),
    )


def lay_kernel(pieces, width, *refs):
    out_ref = refs[-1]
    at = 0
    for first in range(0, len(refs) - 1, pieces):
        for distance in range(pieces):
            part = refs[first + distance]
            owner = jnp.bitwise_xor(position(pieces)[0], distance)
            columns = pl.ds(pl.multiple_of(owner * width + at, LANES), part.shape[1])
            out_ref[:, columns] = part[...]
        at += part.shape[1]


def lay(parts, pieces, width):
    flat = [part for chunk in parts for part in chunk]
    rows = flat[0].shape[0]
    return call(
        functools.partial(lay_kernel, pieces, width),
        "lay_out",
        [*flat],
        [jax.ShapeDtypeStruct((rows, pieces * width), jnp.bfloat16)],
        [],
        cost=(0, 4 * rows * pieces * width, 0),
    )[0]


def swapped(block, apart):
    count = lax.axis_size("row")
    return lax.ppermute(block, "row", [(i, i ^ apart) for i in range(count)])


def on_device(basis, weights):
    axis_len = lax.axis_size("row")
    depth, rows = basis.shape
    pieces = weights.shape[1] // depth
    blocks = axis_len // pieces
    bits = blocks.bit_length() - 1
    step = rows // blocks
    width = weights.shape[2]

    cuts = [0]
    for share, _ in CHUNKS:
        cuts.append(cuts[-1] + share)
    cuts = [cut * (width // LANES) // PARTS * LANES for cut in cuts]
    ahead = cuts[EARLY]
    orders = [[bit for bit in order if bit < bits] for _, order in CHUNKS]
    stages = [split_places(order, bits) for order in orders]
    own, near = prepare(basis, weights, pieces, blocks, bits, ahead)
    left = [own] + [swapped(own, distance) for distance in range(1, pieces)]
    right, partial = early(own, near, weights, pieces, ahead)

    state = {}
    after = [partial]
    finished = {}
    for index, number in ORDER:
        order = orders[index]
        start = cuts[index]
        chunk = cuts[index + 1] - start
        if number == 0:
            begun = partial if index < EARLY else None
            out = product(
                left, right, begun, start, chunk, step, *stages[index][0], after
            )
        elif number < bits:
            message, kept = state[index]
            old = stages[index][number - 1][1]
            out = middle(message, kept, chunk, step, old, *stages[index][number], after)
        else:
            message, kept = state[index]
            out = last(message, kept, chunk, step, pieces, after)
            finished[index] = [out[0]] + [swapped(out[d], d) for d in range(1, pieces)]
            after = [out[0]]
            continue
        state[index] = swapped(out[0], pieces << order[number]), out[1]
        after = [out[1]]
    return lay([finished[index] for index in sorted(finished)], pieces, width)


def solution(mesh):
    in_specs = (P(("groups", "row"), None), P(("groups", "row"), None, None))
    out_specs = P(("groups", "row"), None)
    return jax.shard_map(
        on_device, mesh=mesh, in_specs=in_specs, out_specs=out_specs, check_vma=False
    )
```

```python
import functools

import jax
import jax.numpy as jnp
from jax import lax
from jax.experimental import pallas as pl
from jax.experimental.pallas import tpu as pltpu
from jax.sharding import PartitionSpec as P

LANES = 128
SCALE_ROWS = 16
COLUMNS = 256
TILE = 512
HALF_SPAN = 125.0
SPAN = 250.0
TINY = 2.0**-110
MIB = 1 << 20

CHUNKS = [
    (4, (0, 2, 1)),
    (4, (1, 0, 2)),
    (4, (0, 2, 1)),
    (2, (1, 0, 2)),
    (2, (0, 1, 2)),
]
PARTS = 16
EARLY = 2
ORDER = [
    (0, 0), (1, 0), (2, 0), (0, 1), (3, 0), (4, 0), (1, 1), (2, 1),
    (0, 2), (3, 1), (4, 1), (1, 2), (2, 2), (0, 3), (3, 2), (4, 2),
    (1, 3), (2, 3), (3, 3), (4, 3),
]


def column_bound(values):
    top = jnp.maximum(jnp.max(jnp.abs(values), axis=0, keepdims=True), TINY)
    return (top * 1.008).astype(jnp.bfloat16).astype(jnp.float32)


def encode(values, bound):
    level = jnp.exp2(jnp.abs(values) * (SPAN / bound) - HALF_SPAN)
    return jnp.where(values < 0, -level, level).astype(jnp.bfloat16)


def decode(coded, bound):
    coded = coded.astype(jnp.float32)
    size = (jnp.log2(jnp.abs(coded)) + HALF_SPAN) * (bound * (1.0 / SPAN))
    return jnp.where(coded < 0, -size, size)


def reversed_bits(value, bits):
    out = 0
    for bit in range(bits):
        out |= (value >> bit & 1) << (bits - 1 - bit)
    return out


def split_places(order, bits):
    stay = list(range(1 << bits))
    stages = []
    for bit in order:
        leave = [p for p in stay if reversed_bits(p, bits) >> bit & 1]
        stay = [p for p in stay if not reversed_bits(p, bits) >> bit & 1]
        stages.append((leave, stay))
    return stages


def scale_rows(tiles):
    return -(-tiles // SCALE_ROWS) * SCALE_ROWS


def put_bounds(message_ref, bounds, count):
    tiles = len(bounds)
    spare = scale_rows(tiles) - tiles
    if spare:
        bounds = bounds + [jnp.zeros((spare, LANES), jnp.float32)]
    message_ref[tiles * count :, :] = jnp.concatenate(bounds, axis=0).astype(jnp.bfloat16)


def put_tile(message_ref, kept_ref, tile, blocks, step, leave, stay):
    sent = jnp.concatenate([blocks[p] for p in leave], axis=0)
    bound = column_bound(sent)
    count = len(leave) * step
    message_ref[tile * count : (tile + 1) * count, :] = encode(sent, bound)
    for slot, p in enumerate(stay):
        at = (tile * len(stay) + slot) * step
        kept_ref[at : at + step, :] = blocks[p]
    return bound


def position(pieces):
    me = lax.axis_index("row").astype(jnp.int32)
    return jnp.bitwise_and(me, pieces - 1), jnp.right_shift(me, pieces.bit_length() - 1)


def call(kernel, name, ins, outs, after, scratch=(), limit=4, cost=(0, 0, 0), far=0):
    count = len(ins)

    def run(*refs):
        kernel(*refs[:count], *refs[count + len(after) :])

    vmem = pl.BlockSpec(memory_space=pltpu.VMEM)
    near = count - far
    ins = ins[:near] + [pltpu.with_memory_space_constraint(x, pltpu.HBM) for x in ins[near:]]
    return pl.pallas_call(
        run,
        in_specs=[vmem] * (count - far)
        + [pl.BlockSpec(memory_space=pltpu.HBM)] * far
        + [pl.BlockSpec(memory_space=pl.ANY)] * len(after),
        out_specs=[vmem] * len(outs),
        out_shape=outs,
        scratch_shapes=scratch,
        compiler_params=pltpu.CompilerParams(vmem_limit_bytes=limit * MIB),
        cost_estimate=pl.CostEstimate(flops=1, bytes_accessed=1, transcendentals=0),
        name=name,
    )(*ins, *after)


def row_copies(w_ref, near_ref, sems, pieces, distance, wide, first=0):
    depth, width = near_ref.shape
    owner = jnp.bitwise_xor(position(pieces)[0], distance)
    copies = []
    for index, at in enumerate(range(0, depth, wide)):
        source = pl.ds(pl.multiple_of(owner * depth + at, wide), wide)
        copies.append(
            pltpu.make_async_copy(
                w_ref.at[0, source, pl.ds(first, width)],
                near_ref.at[pl.ds(at, wide), :],
                sems.at[index],
            )
        )
    return copies


def prepare_kernel(
    pieces, blocks, bits, wide, basis_ref, w_ref, out_ref, near_ref, held, turned, sems, w_sems
):
    depth, rows = basis_ref.shape
    step = rows // blocks
    mine = position(pieces)[1]
    copies = []
    for index, at in enumerate(range(0, depth, wide)):
        part = pl.ds(at, wide)
        copies.append(
            pltpu.make_async_copy(basis_ref.at[part, :], held.at[part, :], sems.at[index])
        )
    weight_copies = row_copies(w_ref, near_ref, w_sems, pieces, 0, wide)
    for copy in copies + weight_copies:
        copy.start()
    for index, at in enumerate(range(0, depth, wide)):
        copies[index].wait()
        turned[:, at : at + wide] = held[at : at + wide, :].T
        for place in range(blocks):
            source = jnp.bitwise_xor(mine, reversed_bits(place, bits))
            part = turned[pl.ds(pl.multiple_of(source * step, step), step), at : at + wide]
            high = part.astype(jnp.bfloat16)
            low = (part - high.astype(jnp.float32)).astype(jnp.bfloat16)
            out_ref[place * step : (place + 1) * step, at : at + wide] = high
            out_ref[rows + place * step : rows + (place + 1) * step, at : at + wide] = low
    for copy in weight_copies:
        copy.wait()


def prepare(basis, weights, pieces, blocks, bits, width):
    depth, rows = basis.shape
    wide = min(depth, COLUMNS)
    sems = pltpu.SemaphoreType.DMA((depth // wide,))
    return call(
        functools.partial(prepare_kernel, pieces, blocks, bits, wide),
        "split_basis",
        [basis, weights],
        [
            jax.ShapeDtypeStruct((2 * rows, depth), jnp.bfloat16),
            jax.ShapeDtypeStruct((depth, width), jnp.bfloat16),
        ],
        [],
        [
            pltpu.VMEM((depth, rows), jnp.float32),
            pltpu.VMEM((rows, depth), jnp.float32),
            sems,
            sems,
        ],
        limit=10,
        cost=(2 * depth * rows, 8 * depth * rows, 0),
        far=2,
    )


def spans(width, wide):
    return [(at, min(wide, width - at)) for at in range(0, width, wide)]


def halves_added(product):
    half = product.shape[0] // 2
    return product[:half] + product[half:]


def early_kernel(pieces, width, own_ref, near_ref, w_ref, *refs):
    *later_refs, partial_ref, sems = refs
    depth = own_ref.shape[1]
    wide = min(depth, COLUMNS)
    copies = []
    for distance in [*range(1, pieces), 0]:
        first = 0 if distance else width
        copies += row_copies(
            w_ref, later_refs[distance], sems.at[distance], pieces, distance, wide, first
        )
    for copy in copies:
        copy.start()

    def multiply(columns):
        part = jnp.dot(own_ref[...], near_ref[:, columns], preferred_element_type=jnp.float32)
        partial_ref[:, columns] = halves_added(part)

    turn = 4 * COLUMNS
    turns = width // turn

    def multiply_turn(index):
        for at in range(0, turn, COLUMNS):
            multiply(pl.ds(pl.multiple_of(index * turn + at, COLUMNS), COLUMNS))

    if turns:
        pl.loop(0, turns)(multiply_turn)
    for at, wide in spans(width - turns * turn, COLUMNS):
        multiply(pl.ds(turns * turn + at, wide))
    for copy in copies:
        copy.wait()


def early(own, near, weights, pieces, width):
    rows2, depth = own.shape
    full = weights.shape[2]
    out = call(
        functools.partial(early_kernel, pieces, width),
        "early_products",
        [own, near, weights],
        [jax.ShapeDtypeStruct((depth, full - width), jnp.bfloat16)]
        + [jax.ShapeDtypeStruct((depth, full), jnp.bfloat16)] * (pieces - 1)
        + [jax.ShapeDtypeStruct((rows2 // 2, width), jnp.float32)],
        [],
        [pltpu.SemaphoreType.DMA((pieces, depth // min(depth, COLUMNS)))],
        limit=12,
        cost=(2 * rows2 * depth * width, 2 * pieces * depth * full, 0),
        far=1,
    )
    return out[:-1], out[-1]


def product_kernel(pieces, start, width, skip, early, step, leave, stay, *refs):
    left, right = refs[:pieces], refs[pieces : 2 * pieces]
    message_ref, kept_ref = refs[-2:]
    first = 1 if early else 0
    bounds = []
    for at, wide in spans(width, TILE):
        columns = slice(start + at, start + at + wide)
        own_columns = slice(columns.start - skip, columns.stop - skip)
        taken = [w_ref[:, columns] for w_ref in right[1:]]
        if not early:
            taken = [right[0][:, own_columns]] + taken
        total = jnp.dot(
            jnp.concatenate([a_ref[...] for a_ref in left[first:]], axis=1),
            jnp.concatenate(taken, axis=0),
            preferred_element_type=jnp.float32,
        )
        total = halves_added(total)
        if early:
            total = total + refs[2 * pieces][:, columns]
        for lane in range(0, wide, LANES):
            column = total[:, lane : lane + LANES]
            blocks = {p: column[p * step : (p + 1) * step] for p in leave + stay}
            tile = (at + lane) // LANES
            bounds.append(put_tile(message_ref, kept_ref, tile, blocks, step, leave, stay))
    put_bounds(message_ref, bounds, len(leave) * step)


def outputs(width, step, leave, stay):
    tiles = width // LANES
    sent = tiles * len(leave) * step + scale_rows(tiles)
    return [
        jax.ShapeDtypeStruct((sent, LANES), jnp.bfloat16),
        jax.ShapeDtypeStruct((tiles * len(stay) * step, LANES), jnp.float32),
    ]


def product(left, right, partial, start, width, step, leave, stay, after):
    rows2, depth = left[0].shape
    pieces = len(left)
    early = partial is not None
    skip = right[1].shape[1] - right[0].shape[1]
    count = pieces - 1 if early else pieces
    return call(
        functools.partial(product_kernel, pieces, start, width, skip, early, step, leave, stay),
        "product",
        [*left, *right] + ([partial] if early else []),
        outputs(width, step, leave, stay),
        after,
        limit=12,
        cost=(
            2 * rows2 * depth * count * width,
            2 * depth * count * width + 4 * rows2 * width,
            rows2 * width // 4,
        ),
    )


def received(message_ref, kept_ref, tile, tiles, count):
    coded = message_ref[tile * count : (tile + 1) * count, :]
    group = tile // SCALE_ROWS * SCALE_ROWS
    at = tiles * count + group
    bounds = message_ref[at : at + SCALE_ROWS, :].astype(jnp.float32)
    bound = bounds[tile - group : tile - group + 1]
    return kept_ref[tile * count : (tile + 1) * count, :] + decode(coded, bound)


def middle_kernel(tiles, step, old, leave, stay, message_ref, kept_ref, out_ref, next_ref):
    bounds = []
    for tile in range(tiles):
        column = received(message_ref, kept_ref, tile, tiles, len(old) * step)
        blocks = {p: column[i * step : (i + 1) * step] for i, p in enumerate(old)}
        bounds.append(put_tile(out_ref, next_ref, tile, blocks, step, leave, stay))
    put_bounds(out_ref, bounds, len(leave) * step)


def middle(message, kept, width, step, old, leave, stay, after):
    size = width * len(old) * step
    return call(
        functools.partial(middle_kernel, width // LANES, step, old, leave, stay),
        "add_and_split",
        [message, kept],
        outputs(width, step, leave, stay),
        after,
        cost=(20 * size, 9 * size, 2 * size),
    )


def last_kernel(tiles, pieces, message_ref, kept_ref, *refs):
    outs = refs[:pieces]
    whole = refs[pieces]
    count = whole.shape[0]
    share = count // pieces
    for tile in range(tiles):
        whole[:, tile * LANES : (tile + 1) * LANES] = received(
            message_ref, kept_ref, tile, tiles, count
        )
    for distance in range(pieces):
        owner = jnp.bitwise_xor(position(pieces)[0], distance)
        rows = whole[pl.ds(pl.multiple_of(owner * share, share), share), :]
        outs[distance][...] = rows.astype(jnp.bfloat16)


def last(message, kept, width, step, pieces, after):
    size = width * step
    share = jax.ShapeDtypeStruct((step // pieces, width), jnp.bfloat16)
    return call(
        functools.partial(last_kernel, width // LANES, pieces),
        "add_last",
        [message, kept],
        [share] * pieces,
        after,
        [pltpu.VMEM((step, width), jnp.float32)],
        cost=(10 * size, 8 * size, size),
    )


def lay_kernel(pieces, width, *refs):
    out_ref = refs[-1]
    at = 0
    for first in range(0, len(refs) - 1, pieces):
        for distance in range(pieces):
            part = refs[first + distance]
            owner = jnp.bitwise_xor(position(pieces)[0], distance)
            columns = pl.ds(pl.multiple_of(owner * width + at, LANES), part.shape[1])
            out_ref[:, columns] = part[...]
        at += part.shape[1]


def lay(parts, pieces, width):
    flat = [part for chunk in parts for part in chunk]
    rows = flat[0].shape[0]
    return call(
        functools.partial(lay_kernel, pieces, width),
        "lay_out",
        [*flat],
        [jax.ShapeDtypeStruct((rows, pieces * width), jnp.bfloat16)],
        [],
        cost=(0, 4 * rows * pieces * width, 0),
    )[0]


def swapped(block, apart):
    count = lax.axis_size("row")
    return lax.ppermute(block, "row", [(i, i ^ apart) for i in range(count)])


def on_device(basis, weights):
    axis_len = lax.axis_size("row")
    depth, rows = basis.shape
    pieces = weights.shape[1] // depth
    blocks = axis_len // pieces
    bits = blocks.bit_length() - 1
    step = rows // blocks
    width = weights.shape[2]

    cuts = [0]
    for share, _ in CHUNKS:
        cuts.append(cuts[-1] + share)
    cuts = [cut * (width // LANES) // PARTS * LANES for cut in cuts]
    ahead = cuts[EARLY]
    orders = [[bit for bit in order if bit < bits] for _, order in CHUNKS]
    stages = [split_places(order, bits) for order in orders]
    own, near = prepare(basis, weights, pieces, blocks, bits, ahead)
    left = [own] + [swapped(own, distance) for distance in range(1, pieces)]
    right, partial = early(own, near, weights, pieces, ahead)

    state = {}
    after = [partial]
    finished = {}
    for index, number in ORDER:
        order = orders[index]
        start = cuts[index]
        chunk = cuts[index + 1] - start
        if number == 0:
            begun = partial if index < EARLY else None
            out = product(
                left, right, begun, start, chunk, step, *stages[index][0], after
            )
        elif number < bits:
            message, kept = state[index]
            old = stages[index][number - 1][1]
            out = middle(message, kept, chunk, step, old, *stages[index][number], after)
        else:
            message, kept = state[index]
            out = last(message, kept, chunk, step, pieces, after)
            finished[index] = [out[0]] + [swapped(out[d], d) for d in range(1, pieces)]
            after = [out[0]]
            continue
        state[index] = swapped(out[0], pieces << order[number]), out[1]
        after = [out[1]]
    return lay([finished[index] for index in sorted(finished)], pieces, width)


def solution(mesh):
    in_specs = (P(("groups", "row"), None), P(("groups", "row"), None, None))
    out_specs = P(("groups", "row"), None)
    return jax.shard_map(
        on_device, mesh=mesh, in_specs=in_specs, out_specs=out_specs, check_vma=False
    )
```

```python
import functools

import jax
import jax.numpy as jnp
from jax import lax
from jax.experimental import pallas as pl
from jax.experimental.pallas import tpu as pltpu
from jax.sharding import PartitionSpec as P

LANES = 128
SCALE_ROWS = 16
COLUMNS = 256
TILE = 512
HALF_SPAN = 125.0
SPAN = 250.0
TINY = 2.0**-110
MIB = 1 << 20

CHUNKS = [
    (4, (0, 2, 1)),
    (4, (1, 0, 2)),
    (4, (0, 2, 1)),
    (2, (1, 0, 2)),
    (2, (0, 1, 2)),
]
PARTS = 16
EARLY = 2
ORDER = [
    (0, 0), (1, 0), (2, 0), (0, 1), (3, 0), (4, 0), (1, 1), (2, 1),
    (0, 2), (3, 1), (4, 1), (1, 2), (2, 2), (0, 3), (3, 2), (4, 2),
    (1, 3), (2, 3), (3, 3), (4, 3),
]


def column_bound(values):
    top = jnp.maximum(jnp.max(jnp.abs(values), axis=0, keepdims=True), TINY)
    return (top * 1.008).astype(jnp.bfloat16).astype(jnp.float32)


def encode(values, bound):
    level = jnp.exp2(jnp.abs(values) * (SPAN / bound) - HALF_SPAN)
    return jnp.where(values < 0, -level, level).astype(jnp.bfloat16)


def decode(coded, bound):
    coded = coded.astype(jnp.float32)
    size = (jnp.log2(jnp.abs(coded)) + HALF_SPAN) * (bound * (1.0 / SPAN))
    return jnp.where(coded < 0, -size, size)


def reversed_bits(value, bits):
    out = 0
    for bit in range(bits):
        out |= (value >> bit & 1) << (bits - 1 - bit)
    return out


def split_places(order, bits):
    stay = list(range(1 << bits))
    stages = []
    for bit in order:
        leave = [p for p in stay if reversed_bits(p, bits) >> bit & 1]
        stay = [p for p in stay if not reversed_bits(p, bits) >> bit & 1]
        stages.append((leave, stay))
    return stages


def scale_rows(tiles):
    return -(-tiles // SCALE_ROWS) * SCALE_ROWS


def put_bounds(message_ref, bounds, count):
    tiles = len(bounds)
    spare = scale_rows(tiles) - tiles
    if spare:
        bounds = bounds + [jnp.zeros((spare, LANES), jnp.float32)]
    message_ref[tiles * count :, :] = jnp.concatenate(bounds, axis=0).astype(jnp.bfloat16)


def put_tile(message_ref, kept_ref, tile, blocks, step, leave, stay):
    sent = jnp.concatenate([blocks[p] for p in leave], axis=0)
    bound = column_bound(sent)
    count = len(leave) * step
    message_ref[tile * count : (tile + 1) * count, :] = encode(sent, bound)
    for slot, p in enumerate(stay):
        at = (tile * len(stay) + slot) * step
        kept_ref[at : at + step, :] = blocks[p]
    return bound


def position(pieces):
    me = lax.axis_index("row").astype(jnp.int32)
    return jnp.bitwise_and(me, pieces - 1), jnp.right_shift(me, pieces.bit_length() - 1)


def call(kernel, name, ins, outs, after, scratch=(), limit=4, cost=(0, 0, 0), far=0):
    count = len(ins)

    def run(*refs):
        kernel(*refs[:count], *refs[count + len(after) :])

    vmem = pl.BlockSpec(memory_space=pltpu.VMEM)
    near = count - far
    ins = ins[:near] + [pltpu.with_memory_space_constraint(x, pltpu.HBM) for x in ins[near:]]
    return pl.pallas_call(
        run,
        in_specs=[vmem] * (count - far)
        + [pl.BlockSpec(memory_space=pltpu.HBM)] * far
        + [pl.BlockSpec(memory_space=pl.ANY)] * len(after),
        out_specs=[vmem] * len(outs),
        out_shape=outs,
        scratch_shapes=scratch,
        compiler_params=pltpu.CompilerParams(vmem_limit_bytes=limit * MIB),
        cost_estimate=pl.CostEstimate(flops=1, bytes_accessed=1, transcendentals=0),
        name=name,
    )(*ins, *after)


def row_copies(w_ref, near_ref, sems, pieces, distance, wide, first=0):
    depth, width = near_ref.shape
    owner = jnp.bitwise_xor(position(pieces)[0], distance)
    copies = []
    for index, at in enumerate(range(0, depth, wide)):
        source = pl.ds(pl.multiple_of(owner * depth + at, wide), wide)
        copies.append(
            pltpu.make_async_copy(
                w_ref.at[0, source, pl.ds(first, width)],
                near_ref.at[pl.ds(at, wide), :],
                sems.at[index],
            )
        )
    return copies


def prepare_kernel(
    pieces, blocks, bits, wide, basis_ref, w_ref, out_ref, near_ref, held, turned, sems, w_sems
):
    depth, rows = basis_ref.shape
    step = rows // blocks
    mine = position(pieces)[1]
    copies = []
    for index, at in enumerate(range(0, depth, wide)):
        part = pl.ds(at, wide)
        copies.append(
            pltpu.make_async_copy(basis_ref.at[part, :], held.at[part, :], sems.at[index])
        )
    weight_copies = row_copies(w_ref, near_ref, w_sems, pieces, 0, wide)
    for copy in copies + weight_copies:
        copy.start()
    for index, at in enumerate(range(0, depth, wide)):
        copies[index].wait()
        turned[:, at : at + wide] = held[at : at + wide, :].T
        for place in range(blocks):
            source = jnp.bitwise_xor(mine, reversed_bits(place, bits))
            part = turned[pl.ds(pl.multiple_of(source * step, step), step), at : at + wide]
            high = part.astype(jnp.bfloat16)
            low = (part - high.astype(jnp.float32)).astype(jnp.bfloat16)
            out_ref[place * step : (place + 1) * step, at : at + wide] = high
            out_ref[rows + place * step : rows + (place + 1) * step, at : at + wide] = low
    for copy in weight_copies:
        copy.wait()


def prepare(basis, weights, pieces, blocks, bits, width):
    depth, rows = basis.shape
    wide = min(depth, COLUMNS)
    sems = pltpu.SemaphoreType.DMA((depth // wide,))
    return call(
        functools.partial(prepare_kernel, pieces, blocks, bits, wide),
        "split_basis",
        [basis, weights],
        [
            jax.ShapeDtypeStruct((2 * rows, depth), jnp.bfloat16),
            jax.ShapeDtypeStruct((depth, width), jnp.bfloat16),
        ],
        [],
        [
            pltpu.VMEM((depth, rows), jnp.float32),
            pltpu.VMEM((rows, depth), jnp.float32),
            sems,
            sems,
        ],
        limit=10,
        cost=(2 * depth * rows, 8 * depth * rows, 0),
        far=2,
    )


def spans(width, wide):
    return [(at, min(wide, width - at)) for at in range(0, width, wide)]


def terms(a_ref):
    half = a_ref.shape[0] // 2
    return a_ref[:half, :], a_ref[half:, :]


def halves_added(product):
    half = product.shape[0] // 2
    return product[:half] + product[half:]


def early_kernel(pieces, width, own_ref, near_ref, w_ref, *refs):
    *later_refs, partial_ref, sems = refs
    depth = own_ref.shape[1]
    wide = min(depth, COLUMNS)
    copies = []
    for distance in [*range(1, pieces), 0]:
        first = 0 if distance else width
        copies += row_copies(
            w_ref, later_refs[distance], sems.at[distance], pieces, distance, wide, first
        )
    for copy in copies:
        copy.start()

    def multiply(columns):
        part = jnp.dot(own_ref[...], near_ref[:, columns], preferred_element_type=jnp.float32)
        partial_ref[:, columns] = halves_added(part)

    turn = 4 * COLUMNS
    turns = width // turn

    def multiply_turn(index):
        for at in range(0, turn, COLUMNS):
            multiply(pl.ds(pl.multiple_of(index * turn + at, COLUMNS), COLUMNS))

    if turns:
        pl.loop(0, turns)(multiply_turn)
    for at, wide in spans(width - turns * turn, COLUMNS):
        multiply(pl.ds(turns * turn + at, wide))
    for copy in copies:
        copy.wait()


def early(own, near, weights, pieces, width):
    rows2, depth = own.shape
    full = weights.shape[2]
    out = call(
        functools.partial(early_kernel, pieces, width),
        "early_products",
        [own, near, weights],
        [jax.ShapeDtypeStruct((depth, full - width), jnp.bfloat16)]
        + [jax.ShapeDtypeStruct((depth, full), jnp.bfloat16)] * (pieces - 1)
        + [jax.ShapeDtypeStruct((rows2 // 2, width), jnp.float32)],
        [],
        [pltpu.SemaphoreType.DMA((pieces, depth // min(depth, COLUMNS)))],
        limit=12,
        cost=(2 * rows2 * depth * width, 2 * pieces * depth * full, 0),
        far=1,
    )
    return out[:-1], out[-1]


def product_kernel(pieces, start, width, skip, early, step, leave, stay, *refs):
    left, right = refs[:pieces], refs[pieces : 2 * pieces]
    message_ref, kept_ref = refs[-2:]
    first = 1 if early else 0
    bounds = []
    for at, wide in spans(width, TILE):
        columns = slice(start + at, start + at + wide)
        own_columns = slice(columns.start - skip, columns.stop - skip)
        taken = [w_ref[:, columns] for w_ref in right[1:]]
        if not early:
            taken = [right[0][:, own_columns]] + taken
        total = jnp.dot(
            jnp.concatenate([term for a_ref in left[first:] for term in terms(a_ref)], axis=1),
            jnp.concatenate([rows for rows in taken for _ in range(2)], axis=0),
            preferred_element_type=jnp.float32,
        )
        if early:
            total = total + refs[2 * pieces][:, columns]
        for lane in range(0, wide, LANES):
            column = total[:, lane : lane + LANES]
            blocks = {p: column[p * step : (p + 1) * step] for p in leave + stay}
            tile = (at + lane) // LANES
            bounds.append(put_tile(message_ref, kept_ref, tile, blocks, step, leave, stay))
    put_bounds(message_ref, bounds, len(leave) * step)


def outputs(width, step, leave, stay):
    tiles = width // LANES
    sent = tiles * len(leave) * step + scale_rows(tiles)
    return [
        jax.ShapeDtypeStruct((sent, LANES), jnp.bfloat16),
        jax.ShapeDtypeStruct((tiles * len(stay) * step, LANES), jnp.float32),
    ]


def product(left, right, partial, start, width, step, leave, stay, after):
    rows2, depth = left[0].shape
    pieces = len(left)
    early = partial is not None
    skip = right[1].shape[1] - right[0].shape[1]
    count = pieces - 1 if early else pieces
    return call(
        functools.partial(product_kernel, pieces, start, width, skip, early, step, leave, stay),
        "product",
        [*left, *right] + ([partial] if early else []),
        outputs(width, step, leave, stay),
        after,
        limit=12,
        cost=(
            2 * rows2 * depth * count * width,
            2 * depth * count * width + 4 * rows2 * width,
            rows2 * width // 4,
        ),
    )


def received(message_ref, kept_ref, tile, tiles, count):
    coded = message_ref[tile * count : (tile + 1) * count, :]
    group = tile // SCALE_ROWS * SCALE_ROWS
    at = tiles * count + group
    bounds = message_ref[at : at + SCALE_ROWS, :].astype(jnp.float32)
    bound = bounds[tile - group : tile - group + 1]
    return kept_ref[tile * count : (tile + 1) * count, :] + decode(coded, bound)


def middle_kernel(tiles, step, old, leave, stay, message_ref, kept_ref, out_ref, next_ref):
    bounds = []
    for tile in range(tiles):
        column = received(message_ref, kept_ref, tile, tiles, len(old) * step)
        blocks = {p: column[i * step : (i + 1) * step] for i, p in enumerate(old)}
        bounds.append(put_tile(out_ref, next_ref, tile, blocks, step, leave, stay))
    put_bounds(out_ref, bounds, len(leave) * step)


def middle(message, kept, width, step, old, leave, stay, after):
    size = width * len(old) * step
    return call(
        functools.partial(middle_kernel, width // LANES, step, old, leave, stay),
        "add_and_split",
        [message, kept],
        outputs(width, step, leave, stay),
        after,
        cost=(20 * size, 9 * size, 2 * size),
    )


def last_kernel(tiles, pieces, message_ref, kept_ref, *refs):
    outs = refs[:pieces]
    whole = refs[pieces]
    count = whole.shape[0]
    share = count // pieces
    for tile in range(tiles):
        whole[:, tile * LANES : (tile + 1) * LANES] = received(
            message_ref, kept_ref, tile, tiles, count
        )
    for distance in range(pieces):
        owner = jnp.bitwise_xor(position(pieces)[0], distance)
        rows = whole[pl.ds(pl.multiple_of(owner * share, share), share), :]
        outs[distance][...] = rows.astype(jnp.bfloat16)


def last(message, kept, width, step, pieces, after):
    size = width * step
    share = jax.ShapeDtypeStruct((step // pieces, width), jnp.bfloat16)
    return call(
        functools.partial(last_kernel, width // LANES, pieces),
        "add_last",
        [message, kept],
        [share] * pieces,
        after,
        [pltpu.VMEM((step, width), jnp.float32)],
        cost=(10 * size, 8 * size, size),
    )


def lay_kernel(pieces, width, *refs):
    out_ref = refs[-1]
    at = 0
    for first in range(0, len(refs) - 1, pieces):
        for distance in range(pieces):
            part = refs[first + distance]
            owner = jnp.bitwise_xor(position(pieces)[0], distance)
            columns = pl.ds(pl.multiple_of(owner * width + at, LANES), part.shape[1])
            out_ref[:, columns] = part[...]
        at += part.shape[1]


def lay(parts, pieces, width):
    flat = [part for chunk in parts for part in chunk]
    rows = flat[0].shape[0]
    return call(
        functools.partial(lay_kernel, pieces, width),
        "lay_out",
        [*flat],
        [jax.ShapeDtypeStruct((rows, pieces * width), jnp.bfloat16)],
        [],
        cost=(0, 4 * rows * pieces * width, 0),
    )[0]


def swapped(block, apart):
    count = lax.axis_size("row")
    return lax.ppermute(block, "row", [(i, i ^ apart) for i in range(count)])


def on_device(basis, weights):
    axis_len = lax.axis_size("row")
    depth, rows = basis.shape
    pieces = weights.shape[1] // depth
    blocks = axis_len // pieces
    bits = blocks.bit_length() - 1
    step = rows // blocks
    width = weights.shape[2]

    cuts = [0]
    for share, _ in CHUNKS:
        cuts.append(cuts[-1] + share)
    cuts = [cut * (width // LANES) // PARTS * LANES for cut in cuts]
    ahead = cuts[EARLY]
    orders = [[bit for bit in order if bit < bits] for _, order in CHUNKS]
    stages = [split_places(order, bits) for order in orders]
    own, near = prepare(basis, weights, pieces, blocks, bits, ahead)
    left = [own] + [swapped(own, distance) for distance in range(1, pieces)]
    right, partial = early(own, near, weights, pieces, ahead)

    state = {}
    after = [partial]
    finished = {}
    for index, number in ORDER:
        order = orders[index]
        start = cuts[index]
        chunk = cuts[index + 1] - start
        if number == 0:
            begun = partial if index < EARLY else None
            out = product(
                left, right, begun, start, chunk, step, *stages[index][0], after
            )
        elif number < bits:
            message, kept = state[index]
            old = stages[index][number - 1][1]
            out = middle(message, kept, chunk, step, old, *stages[index][number], after)
        else:
            message, kept = state[index]
            out = last(message, kept, chunk, step, pieces, after)
            finished[index] = [out[0]] + [swapped(out[d], d) for d in range(1, pieces)]
            after = [out[0]]
            continue
        state[index] = swapped(out[0], pieces << order[number]), out[1]
        after = [out[1]]
    return lay([finished[index] for index in sorted(finished)], pieces, width)


def solution(mesh):
    in_specs = (P(("groups", "row"), None), P(("groups", "row"), None, None))
    out_specs = P(("groups", "row"), None)
    return jax.shard_map(
        on_device, mesh=mesh, in_specs=in_specs, out_specs=out_specs, check_vma=False
    )
```

```python
import functools

import jax
import jax.numpy as jnp
from jax import lax
from jax.experimental import pallas as pl
from jax.experimental.pallas import tpu as pltpu
from jax.sharding import PartitionSpec as P

LANES = 128
SCALE_ROWS = 16
COLUMNS = 256
TILE = 512
HALF_SPAN = 125.0
SPAN = 250.0
TINY = 2.0**-110
MIB = 1 << 20

CHUNKS = [
    (4, (0, 2, 1)),
    (4, (1, 0, 2)),
    (4, (0, 2, 1)),
    (2, (1, 0, 2)),
    (2, (0, 1, 2)),
]
PARTS = 16
EARLY = 2
ORDER = [
    (0, 0), (1, 0), (2, 0), (0, 1), (3, 0), (4, 0), (1, 1), (2, 1),
    (0, 2), (3, 1), (4, 1), (1, 2), (2, 2), (0, 3), (3, 2), (4, 2),
    (1, 3), (2, 3), (3, 3), (4, 3),
]


def column_bound(values):
    top = jnp.maximum(jnp.max(jnp.abs(values), axis=0, keepdims=True), TINY)
    return (top * 1.008).astype(jnp.bfloat16).astype(jnp.float32)


def encode(values, bound):
    level = jnp.exp2(jnp.abs(values) * (SPAN / bound) - HALF_SPAN)
    return jnp.where(values < 0, -level, level).astype(jnp.bfloat16)


def decode(coded, bound):
    coded = coded.astype(jnp.float32)
    size = (jnp.log2(jnp.abs(coded)) + HALF_SPAN) * (bound * (1.0 / SPAN))
    return jnp.where(coded < 0, -size, size)


def reversed_bits(value, bits):
    out = 0
    for bit in range(bits):
        out |= (value >> bit & 1) << (bits - 1 - bit)
    return out


def split_places(order, bits):
    stay = list(range(1 << bits))
    stages = []
    for bit in order:
        leave = [p for p in stay if reversed_bits(p, bits) >> bit & 1]
        stay = [p for p in stay if not reversed_bits(p, bits) >> bit & 1]
        stages.append((leave, stay))
    return stages


def scale_rows(tiles):
    return -(-tiles // SCALE_ROWS) * SCALE_ROWS


def put_bounds(message_ref, bounds, count):
    tiles = len(bounds)
    spare = scale_rows(tiles) - tiles
    if spare:
        bounds = bounds + [jnp.zeros((spare, LANES), jnp.float32)]
    message_ref[tiles * count :, :] = jnp.concatenate(bounds, axis=0).astype(jnp.bfloat16)


def put_tile(message_ref, kept_ref, tile, blocks, step, leave, stay):
    sent = jnp.concatenate([blocks[p] for p in leave], axis=0)
    bound = column_bound(sent)
    count = len(leave) * step
    message_ref[tile * count : (tile + 1) * count, :] = encode(sent, bound)
    for slot, p in enumerate(stay):
        at = (tile * len(stay) + slot) * step
        kept_ref[at : at + step, :] = blocks[p]
    return bound


def position(pieces):
    me = lax.axis_index("row").astype(jnp.int32)
    return jnp.bitwise_and(me, pieces - 1), jnp.right_shift(me, pieces.bit_length() - 1)


def call(kernel, name, ins, outs, after, scratch=(), limit=4, cost=(0, 0, 0), far=0):
    count = len(ins)

    def run(*refs):
        kernel(*refs[:count], *refs[count + len(after) :])

    vmem = pl.BlockSpec(memory_space=pltpu.VMEM)
    near = count - far
    ins = ins[:near] + [pltpu.with_memory_space_constraint(x, pltpu.HBM) for x in ins[near:]]
    return pl.pallas_call(
        run,
        in_specs=[vmem] * (count - far)
        + [pl.BlockSpec(memory_space=pltpu.HBM)] * far
        + [pl.BlockSpec(memory_space=pl.ANY)] * len(after),
        out_specs=[vmem] * len(outs),
        out_shape=outs,
        scratch_shapes=scratch,
        compiler_params=pltpu.CompilerParams(vmem_limit_bytes=limit * MIB),
        cost_estimate=pl.CostEstimate(flops=1, bytes_accessed=1, transcendentals=0),
        name=name,
    )(*ins, *after)


def row_copies(w_ref, near_ref, sems, pieces, distance, wide, first=0):
    depth, width = near_ref.shape
    owner = jnp.bitwise_xor(position(pieces)[0], distance)
    copies = []
    for index, at in enumerate(range(0, depth, wide)):
        source = pl.ds(pl.multiple_of(owner * depth + at, wide), wide)
        copies.append(
            pltpu.make_async_copy(
                w_ref.at[0, source, pl.ds(first, width)],
                near_ref.at[pl.ds(at, wide), :],
                sems.at[index],
            )
        )
    return copies


def prepare_kernel(
    pieces, blocks, bits, wide, basis_ref, w_ref, out_ref, near_ref, held, turned, sems, w_sems
):
    depth, rows = basis_ref.shape
    step = rows // blocks
    mine = position(pieces)[1]
    copies = []
    for index, at in enumerate(range(0, depth, wide)):
        part = pl.ds(at, wide)
        copies.append(
            pltpu.make_async_copy(basis_ref.at[part, :], held.at[part, :], sems.at[index])
        )
    weight_copies = row_copies(w_ref, near_ref, w_sems, pieces, 0, wide)
    for copy in copies + weight_copies:
        copy.start()
    for index, at in enumerate(range(0, depth, wide)):
        copies[index].wait()
        turned[:, at : at + wide] = held[at : at + wide, :].T
        for place in range(blocks):
            source = jnp.bitwise_xor(mine, reversed_bits(place, bits))
            part = turned[pl.ds(pl.multiple_of(source * step, step), step), at : at + wide]
            high = part.astype(jnp.bfloat16)
            low = (part - high.astype(jnp.float32)).astype(jnp.bfloat16)
            out_ref[place * step : (place + 1) * step, at : at + wide] = high
            out_ref[rows + place * step : rows + (place + 1) * step, at : at + wide] = low
    for copy in weight_copies:
        copy.wait()


def prepare(basis, weights, pieces, blocks, bits, width):
    depth, rows = basis.shape
    wide = min(depth, COLUMNS)
    sems = pltpu.SemaphoreType.DMA((depth // wide,))
    return call(
        functools.partial(prepare_kernel, pieces, blocks, bits, wide),
        "split_basis",
        [basis, weights],
        [
            jax.ShapeDtypeStruct((2 * rows, depth), jnp.bfloat16),
            jax.ShapeDtypeStruct((depth, width), jnp.bfloat16),
        ],
        [],
        [
            pltpu.VMEM((depth, rows), jnp.float32),
            pltpu.VMEM((rows, depth), jnp.float32),
            sems,
            sems,
        ],
        limit=10,
        cost=(2 * depth * rows, 8 * depth * rows, 0),
        far=2,
    )


def spans(width, wide):
    return [(at, min(wide, width - at)) for at in range(0, width, wide)]


def halves_added(product):
    half = product.shape[0] // 2
    return product[:half] + product[half:]


def early_kernel(pieces, width, own_ref, near_ref, w_ref, *refs):
    *later_refs, partial_ref, sems = refs
    depth = own_ref.shape[1]
    wide = min(depth, COLUMNS)
    copies = []
    for distance in [*range(1, pieces), 0]:
        first = 0 if distance else width
        copies += row_copies(
            w_ref, later_refs[distance], sems.at[distance], pieces, distance, wide, first
        )
    for copy in copies:
        copy.start()

    def multiply(columns):
        part = jnp.dot(own_ref[...], near_ref[:, columns], preferred_element_type=jnp.float32)
        partial_ref[:, columns] = halves_added(part)

    turn = 4 * COLUMNS
    turns = width // turn

    def multiply_turn(index):
        for at in range(0, turn, COLUMNS):
            multiply(pl.ds(pl.multiple_of(index * turn + at, COLUMNS), COLUMNS))

    if turns:
        pl.loop(0, turns)(multiply_turn)
    for at, wide in spans(width - turns * turn, COLUMNS):
        multiply(pl.ds(turns * turn + at, wide))
    for copy in copies:
        copy.wait()


def early(own, near, weights, pieces, width):
    rows2, depth = own.shape
    full = weights.shape[2]
    out = call(
        functools.partial(early_kernel, pieces, width),
        "early_products",
        [own, near, weights],
        [jax.ShapeDtypeStruct((depth, full - width), jnp.bfloat16)]
        + [jax.ShapeDtypeStruct((depth, full), jnp.bfloat16)] * (pieces - 1)
        + [jax.ShapeDtypeStruct((rows2 // 2, width), jnp.float32)],
        [],
        [pltpu.SemaphoreType.DMA((pieces, depth // min(depth, COLUMNS)))],
        limit=12,
        cost=(2 * rows2 * depth * width, 2 * pieces * depth * full, 0),
        far=1,
    )
    return out[:-1], out[-1]


def product_kernel(pieces, start, width, skip, early, step, leave, stay, *refs):
    left, right = refs[:pieces], refs[pieces : 2 * pieces]
    message_ref, kept_ref = refs[-2:]
    first = 1 if early else 0
    bounds = []
    for at, wide in spans(width, TILE):
        columns = slice(start + at, start + at + wide)
        own_columns = slice(columns.start - skip, columns.stop - skip)
        taken = [w_ref[:, columns] for w_ref in right[1:]]
        if not early:
            taken = [right[0][:, own_columns]] + taken
        total = jnp.dot(
            jnp.concatenate([a_ref[...] for a_ref in left[first:]], axis=1),
            jnp.concatenate(taken, axis=0),
            preferred_element_type=jnp.float32,
        )
        total = halves_added(total)
        if early:
            total = total + refs[2 * pieces][:, columns]
        for lane in range(0, wide, LANES):
            column = total[:, lane : lane + LANES]
            blocks = {p: column[p * step : (p + 1) * step] for p in leave + stay}
            tile = (at + lane) // LANES
            bounds.append(put_tile(message_ref, kept_ref, tile, blocks, step, leave, stay))
    put_bounds(message_ref, bounds, len(leave) * step)


def outputs(width, step, leave, stay):
    tiles = width // LANES
    sent = tiles * len(leave) * step + scale_rows(tiles)
    return [
        jax.ShapeDtypeStruct((sent, LANES), jnp.bfloat16),
        jax.ShapeDtypeStruct((tiles * len(stay) * step, LANES), jnp.float32),
    ]


def product(left, right, partial, start, width, step, leave, stay, after):
    rows2, depth = left[0].shape
    pieces = len(left)
    early = partial is not None
    skip = right[1].shape[1] - right[0].shape[1]
    count = pieces - 1 if early else pieces
    return call(
        functools.partial(product_kernel, pieces, start, width, skip, early, step, leave, stay),
        "product",
        [*left, *right] + ([partial] if early else []),
        outputs(width, step, leave, stay),
        after,
        limit=12,
        cost=(
            2 * rows2 * depth * count * width,
            2 * depth * count * width + 4 * rows2 * width,
            rows2 * width // 4,
        ),
    )


def received(message_ref, kept_ref, tile, tiles, count):
    coded = message_ref[tile * count : (tile + 1) * count, :]
    group = tile // SCALE_ROWS * SCALE_ROWS
    at = tiles * count + group
    bounds = message_ref[at : at + SCALE_ROWS, :].astype(jnp.float32)
    bound = bounds[tile - group : tile - group + 1]
    return kept_ref[tile * count : (tile + 1) * count, :] + decode(coded, bound)


def middle_kernel(tiles, step, old, leave, stay, message_ref, kept_ref, out_ref, next_ref):
    bounds = []
    for tile in range(tiles):
        column = received(message_ref, kept_ref, tile, tiles, len(old) * step)
        blocks = {p: column[i * step : (i + 1) * step] for i, p in enumerate(old)}
        bounds.append(put_tile(out_ref, next_ref, tile, blocks, step, leave, stay))
    put_bounds(out_ref, bounds, len(leave) * step)


def middle(message, kept, width, step, old, leave, stay, after):
    size = width * len(old) * step
    return call(
        functools.partial(middle_kernel, width // LANES, step, old, leave, stay),
        "add_and_split",
        [message, kept],
        outputs(width, step, leave, stay),
        after,
        cost=(20 * size, 9 * size, 2 * size),
    )


def last_kernel(tiles, pieces, message_ref, kept_ref, *refs):
    outs = refs[:pieces]
    whole = refs[pieces]
    count = whole.shape[0]
    share = count // pieces
    for tile in range(tiles):
        whole[:, tile * LANES : (tile + 1) * LANES] = received(
            message_ref, kept_ref, tile, tiles, count
        )
    for distance in range(pieces):
        owner = jnp.bitwise_xor(position(pieces)[0], distance)
        rows = whole[pl.ds(pl.multiple_of(owner * share, share), share), :]
        outs[distance][...] = rows.astype(jnp.bfloat16)


def last(message, kept, width, step, pieces, after):
    size = width * step
    share = jax.ShapeDtypeStruct((step // pieces, width), jnp.bfloat16)
    return call(
        functools.partial(last_kernel, width // LANES, pieces),
        "add_last",
        [message, kept],
        [share] * pieces,
        after,
        [pltpu.VMEM((step, width), jnp.float32)],
        cost=(10 * size, 8 * size, size),
    )


def lay_kernel(pieces, width, *refs):
    *parts, out_ref, sems = refs
    copies = []
    at = 0
    for first in range(0, len(parts), pieces):
        for distance in range(pieces):
            part = parts[first + distance]
            owner = jnp.bitwise_xor(position(pieces)[0], distance)
            columns = pl.ds(pl.multiple_of(owner * width + at, LANES), part.shape[1])
            copies.append(
                pltpu.make_async_copy(part, out_ref.at[:, columns], sems.at[len(copies)])
            )
        at += part.shape[1]
    for copy in copies:
        copy.start()
    for copy in copies:
        copy.wait()


def lay(parts, pieces, width):
    flat = [part for chunk in parts for part in chunk]
    rows = flat[0].shape[0]
    return pl.pallas_call(
        functools.partial(lay_kernel, pieces, width),
        in_specs=[pl.BlockSpec(memory_space=pltpu.VMEM)] * len(flat),
        out_specs=pl.BlockSpec(memory_space=pltpu.HBM),
        out_shape=jax.ShapeDtypeStruct((rows, pieces * width), jnp.bfloat16),
        scratch_shapes=[pltpu.SemaphoreType.DMA((len(flat),))],
        compiler_params=pltpu.CompilerParams(vmem_limit_bytes=4 * MIB),
        cost_estimate=pl.CostEstimate(flops=1, bytes_accessed=1, transcendentals=0),
        name="lay_out",
    )(*flat)


def swapped(block, apart):
    count = lax.axis_size("row")
    return lax.ppermute(block, "row", [(i, i ^ apart) for i in range(count)])


def on_device(basis, weights):
    axis_len = lax.axis_size("row")
    depth, rows = basis.shape
    pieces = weights.shape[1] // depth
    blocks = axis_len // pieces
    bits = blocks.bit_length() - 1
    step = rows // blocks
    width = weights.shape[2]

    cuts = [0]
    for share, _ in CHUNKS:
        cuts.append(cuts[-1] + share)
    cuts = [cut * (width // LANES) // PARTS * LANES for cut in cuts]
    ahead = cuts[EARLY]
    orders = [[bit for bit in order if bit < bits] for _, order in CHUNKS]
    stages = [split_places(order, bits) for order in orders]
    own, near = prepare(basis, weights, pieces, blocks, bits, ahead)
    left = [own] + [swapped(own, distance) for distance in range(1, pieces)]
    right, partial = early(own, near, weights, pieces, ahead)

    state = {}
    after = [partial]
    finished = {}
    for index, number in ORDER:
        order = orders[index]
        start = cuts[index]
        chunk = cuts[index + 1] - start
        if number == 0:
            begun = partial if index < EARLY else None
            out = product(
                left, right, begun, start, chunk, step, *stages[index][0], after
            )
        elif number < bits:
            message, kept = state[index]
            old = stages[index][number - 1][1]
            out = middle(message, kept, chunk, step, old, *stages[index][number], after)
        else:
            message, kept = state[index]
            out = last(message, kept, chunk, step, pieces, after)
            finished[index] = [out[0]] + [swapped(out[d], d) for d in range(1, pieces)]
            after = [out[0]]
            continue
        state[index] = swapped(out[0], pieces << order[number]), out[1]
        after = [out[1]]
    return lay([finished[index] for index in sorted(finished)], pieces, width)


def solution(mesh):
    in_specs = (P(("groups", "row"), None), P(("groups", "row"), None, None))
    out_specs = P(("groups", "row"), None)
    return jax.shard_map(
        on_device, mesh=mesh, in_specs=in_specs, out_specs=out_specs, check_vma=False
    )
```
